32 devices in a mesh: dev: 32 (over z, y, x, core).
Axes of the slice: x: 2, y: 2, z: 4, core: 2. Of those that a mesh axis runs over, the one named last changes fastest.
Arguments:
- saved: bfloat16 [32, 1024, 768], P('dev'), may hold values from -6 to 6
- cotangent: bfloat16 [32, 1024, 2048], P('dev'), may hold values from -6 to 6
- weights: bfloat16 [32, 768, 2048], P('dev'), may hold values from -0.21875 to 0.21875
- counts: int32 [16], replicated, may hold values from 1 to 8, as said below
- live_rows: int32 [32], P('dev'), may hold values from 1 to 1024, 20480 in all
- next_map: int32 [32], replicated, may hold values from 0 to 15, as said below
- master: float32 [16, 768, 2048], P(None, 'dev'), may hold values from -0.21875 to 0.21875
- moment1: bfloat16 [16, 768, 2048], P(None, 'dev'), may hold values from -6 to 6
- moment2: bfloat16 [16, 768, 2048], P(None, 'dev'), may hold values from 0.049804688 to 4
Outputs:
- input_grads: bfloat16 [32, 1024, 768], P('dev')
- master_out: float32 [16, 768, 2048], P(None, 'dev')
- moment1_out: bfloat16 [16, 768, 2048], P(None, 'dev')
- moment2_out: bfloat16 [16, 768, 2048], P(None, 'dev')
- next_weights: bfloat16 [32, 768, 2048], P('dev')
The draws below stay inside these ranges and needn't reach their ends.
Inputs may be any that keep to these rules, and one draw needn't show every extreme that they name: The counts sum to 32; in the current placement expert e holds the counts[e] slots that follow those of experts below e; some expert has exactly 8 replicas. `next_map`: every expert is named by 1 to 8 slots; some expert by exactly 8. `live_rows`: the live rows of all slots sum to 20480, and some slot has exactly 1024.
All inputs are finite; a program needn't handle non-finite values. No bound on the sum of `live_rows` on one device may be relied on, other than what follows from the above.
Results may differ from the reference program's by a relative error of at most 0.0058.
Values may be sent and summed in bfloat16 or wider, within the bound.
A program may use at most 128 MiB of HBM per device.

```python
import math
import jax
import jax.numpy as jnp
import numpy as np
from jax import lax

D = 2048
HID = 768
ROWS = 1024
SLOTS = 32
EXPERTS = 16


def replica_counts(key):
    shuffled = jax.random.permutation(jax.random.fold_in(key, 1), EXPERTS).astype(jnp.int32)
    ranking = jnp.zeros((EXPERTS,), jnp.int32).at[shuffled].set(jnp.arange(EXPERTS, dtype=jnp.int32))
    initial = jnp.ones((EXPERTS,), jnp.int32).at[shuffled[0]].set(8)

    def place(number, current):
        priority = jax.random.randint(jax.random.fold_in(key, 100 + number), (EXPERTS,), 0, 1 << 20) // (1 + ranking)
        priority = jnp.where((current < 8) & (ranking > 0), priority, -1)
        return current.at[jnp.argmax(priority)].add(1)
    return lax.fori_loop(0, SLOTS - EXPERTS - 7, place, initial)


def draw_counts(key, part):
    return replica_counts(jax.random.fold_in(key, 11)).astype(jnp.int32)


def draw_next_map(key, part):
    tally = replica_counts(jax.random.fold_in(key, 22))
    bounds = jnp.cumsum(tally)
    slot_index = jnp.arange(SLOTS, dtype=jnp.int32)
    owners = jnp.sum((bounds[None, :] <= slot_index[:, None]).astype(jnp.int32), axis=1)
    shuffle = jax.random.permutation(jax.random.fold_in(key, 33), SLOTS)
    return owners[shuffle].astype(jnp.int32)


def levels(key, shape, pieces, least, largest):
    def one(position, blocks):
        heights = jax.random.uniform(jax.random.fold_in(jax.random.fold_in(key, 6), position), (blocks,), jnp.float32, least / len(pieces), largest / len(pieces))
        return jnp.repeat(jnp.exp(heights), shape[position] // blocks).reshape((-1,) + (1,) * (len(shape) - position - 1))

    level = one(*pieces[0])
    for cut in pieces[1:]:
        level = level * one(*cut)
    return level


def profile(amount, total, most, slope):
    loads = [(1 << 20) // math.isqrt(rank ** slope) + 1 for rank in range(2, amount + 1)]
    rest, given = total - most - (amount - 1), [1] * (amount - 1)
    while rest > 0:
        candidates = [i for i in range(amount - 1) if given[i] < most]
        pool, remaining = sum([loads[i] for i in candidates]), rest
        for i in candidates:
            extra = min(most - given[i], max(1, remaining * loads[i] // pool), rest)
            given[i] = given[i] + extra
            rest = rest - extra
    return np.array([most] + given)


def ragged_sizes(key, number_of, total, reach, skew):
    if number_of == 2:
        one = jax.random.randint(key, (), max(1, total - reach), min(reach, total - 1) + 1)
        return jnp.stack([one, total - one])
    lengths = jnp.asarray(profile(number_of, total, reach, skew), jnp.int32)
    couples = (number_of - 1) // 2
    source_of, sink = lengths[1:1 + 2 * couples:2], lengths[2:2 + 2 * couples:2]
    slack = jnp.minimum(source_of - 1, reach - sink)
    passed = jax.random.randint(jax.random.fold_in(key, 1), (couples,), 0, 1 << 20) % (slack + 1)
    lengths = lengths.at[1:1 + 2 * couples:2].set(source_of - passed).at[2:2 + 2 * couples:2].set(sink + passed)
    return lengths[jax.random.permutation(jax.random.fold_in(key, 2), number_of)]


def bell_draw(key, extent, deviation, reach, pieces=(), kind=jnp.bfloat16):
    values = deviation * jax.random.normal(key, extent, jnp.float32)
    if pieces:
        values = values * levels(key, extent, pieces, -0.22, 0.18)
    return jnp.clip(values, -reach, reach).astype(kind)


def setup_inputs(seed: int = 0) -> dict:
    streams_of = jax.random.split(jax.random.key(seed), 10)
    saved = bell_draw(streams_of[0], (SLOTS, ROWS, HID), 1.0, 6.0, ((0, 32),))
    cotangent = bell_draw(streams_of[1], (SLOTS, ROWS, D), 1.0, 6.0, ((0, 32),))
    weights = bell_draw(streams_of[2], (SLOTS, HID, D), HID ** -0.5, 0.21875, ((0, 32),))
    counts = draw_counts(jax.random.fold_in(streams_of[9], 71), 0)
    live_rows = ragged_sizes(streams_of[4], SLOTS, SLOTS * ROWS * 5 // 8, ROWS, 2).astype(jnp.int32)
    next_map = draw_next_map(jax.random.fold_in(streams_of[9], 71), 0)
    master = bell_draw(streams_of[6], (EXPERTS, HID, D), HID ** -0.5, 0.21875, ((1, 32),), jnp.float32)
    moment1 = bell_draw(streams_of[7], (EXPERTS, HID, D), 1.0, 6.0, ((1, 32),))
    moment2 = jnp.clip(jnp.exp(math.log(4.0) - 4.3859405 * jax.random.uniform(streams_of[8], (EXPERTS, HID, D), jnp.float32) ** levels(streams_of[8], (EXPERTS, HID, D), ((1, 32),), -0.2, 0.2)), 0.049804688, 4.0).astype(jnp.bfloat16)
    return dict(saved=saved, cotangent=cotangent, weights=weights, counts=counts, live_rows=live_rows, next_map=next_map, master=master, moment1=moment1, moment2=moment2)


LEARN_RATE = 0.001
DECAY_RATE = 0.1
BETA_ONE = 0.9
BETA_TWO = 0.95
BIAS_ONE = 1.0 - 0.9 ** 20
BIAS_TWO = 1.0 - 0.95 ** 20
EPSILON = 1e-08

def reference(saved, cotangent, weights, counts, live_rows, next_map, master, moment1, moment2):
    bounds = jnp.cumsum(counts).astype(jnp.int32)
    slot_index = jnp.arange(SLOTS, dtype=jnp.int32)
    holders = lax.optimization_barrier(jnp.sum((bounds[None, :] <= slot_index[:, None]).astype(jnp.int32), axis=1)).astype(jnp.int32)
    row_index = jnp.arange(ROWS, dtype=jnp.int32)

    def per_slot(totals, inputs):
        hidden_rows, cot_rows, slot_weights, expert, live_count = inputs
        masked = jnp.where((row_index < live_count)[:, None], cot_rows, jnp.zeros_like(cot_rows))
        grads_in = jnp.dot(masked, slot_weights.T, preferred_element_type=jnp.float32).astype(jnp.bfloat16)
        slot_grads = jnp.dot(hidden_rows.T, masked, preferred_element_type=jnp.float32).astype(jnp.bfloat16)
        totals = totals.at[expert].add(slot_grads.astype(jnp.float32))
        return (totals, grads_in)
    empty = jnp.zeros((EXPERTS, HID, D), jnp.float32)
    expert_grads, input_grads = lax.scan(per_slot, empty, (saved, cotangent, weights, holders, live_rows))
    first = BETA_ONE * moment1.astype(jnp.float32) + (1.0 - BETA_ONE) * expert_grads
    second = BETA_TWO * moment2.astype(jnp.float32) + (1.0 - BETA_TWO) * expert_grads * expert_grads
    update = first / BIAS_ONE / (jnp.sqrt(second / BIAS_TWO) + EPSILON) + DECAY_RATE * master
    master_out = master - LEARN_RATE * update
    next_weights = jnp.take(master_out.astype(jnp.bfloat16), next_map, axis=0)
    return (input_grads, master_out, first.astype(jnp.bfloat16), second.astype(jnp.bfloat16), next_weights)
```

```python
import functools

import jax
import jax.numpy as jnp
from jax import lax
from jax.experimental import pallas as pl
from jax.experimental.pallas import tpu as pltpu
from jax.sharding import PartitionSpec as P

LEARN_RATE = 0.001
DECAY_RATE = 0.1
BETA_ONE = 0.9
BETA_TWO = 0.95
BIAS_ONE = 1.0 - 0.9**20
BIAS_TWO = 1.0 - 0.95**20
EPSILON = 1e-08
GROUP = 8
CHUNKS = 4
MOST = 8
MESH = pl.DeviceIdType.MESH


def contract_rows(left, right):
    return lax.dot_general(
        left, right, (((0,), (0,)), ((), ())), preferred_element_type=jnp.float32
    )


def contract_cols(left, right):
    return lax.dot_general(
        left, right, (((1,), (1,)), ((), ())), preferred_element_type=jnp.float32
    )


def adam(grads, master, moment1, moment2):
    first = BETA_ONE * moment1 + (1.0 - BETA_ONE) * grads
    second = BETA_TWO * moment2 + (1.0 - BETA_TWO) * grads * grads
    update = first / BIAS_ONE / (jnp.sqrt(second / BIAS_TWO) + EPSILON) + DECAY_RATE * master
    return master - LEARN_RATE * update, first, second


def plain(saved, cotangent, weights, counts, live_rows, next_map, master, moment1, moment2):
    hidden_rows, cot_rows, slot_weights = saved[0], cotangent[0], weights[0]
    devices = lax.axis_size("dev")
    expert_count, share_rows, model_width = master.shape
    row_index = jnp.arange(hidden_rows.shape[0], dtype=jnp.int32)
    masked = jnp.where((row_index < live_rows[0])[:, None], cot_rows, jnp.zeros_like(cot_rows))
    input_grads = contract_cols(masked, slot_weights).astype(jnp.bfloat16)
    slot_grads = contract_rows(hidden_rows, masked).astype(jnp.bfloat16)
    slot_index = jnp.arange(devices, dtype=jnp.int32)
    bounds = jnp.cumsum(counts)
    holders = jnp.sum((bounds[None, :] <= slot_index[:, None]).astype(jnp.int32), axis=1)
    selector = (jnp.arange(expert_count, dtype=jnp.int32)[:, None] == holders[None, :]).astype(
        jnp.bfloat16
    )
    received = lax.all_to_all(slot_grads, "dev", split_axis=0, concat_axis=0, tiled=True)
    pieces = received.reshape(devices, share_rows, model_width)
    expert_grads = jnp.einsum("es,src->erc", selector, pieces, preferred_element_type=jnp.float32)
    master_out, first, second = adam(
        expert_grads, master, moment1.astype(jnp.float32), moment2.astype(jnp.float32)
    )
    outgoing = jnp.take(master_out.astype(jnp.bfloat16), next_map, axis=0)
    outgoing = outgoing.reshape(devices * share_rows, model_width)
    arriving = lax.all_to_all(outgoing, "dev", split_axis=0, concat_axis=0, tiled=True)
    return (
        input_grads[None],
        master_out,
        first.astype(jnp.bfloat16),
        second.astype(jnp.bfloat16),
        arriving[None],
    )


def tables(counts, next_map, devices):
    planes, experts = devices // GROUP, counts.shape[0]
    lane = jnp.arange(GROUP, dtype=jnp.int32)
    slot = jnp.arange(devices, dtype=jnp.int32)
    ids = jnp.arange(experts, dtype=jnp.int32)
    bounds = jnp.sum(jnp.where(ids[None, :] <= ids[:, None], counts[None, :], 0), axis=1)
    holders = jnp.sum((bounds[None, :] <= slot[:, None]).astype(jnp.int32), axis=1)
    held = holders.reshape(planes, GROUP)
    same = held[:, :, None] == held[:, None, :]
    earlier = lane[None, :] < lane[:, None]
    cont = jnp.any(same & earlier[None], axis=2)
    rank = jnp.sum((~cont[:, None, :]) & (lane[None, :] <= lane[:, None])[None], axis=2) - 1
    at_rank = rank[:, None, :] == lane[None, :, None]
    last = jnp.max(jnp.where(at_rank, lane[None, None, :], 0), axis=2)
    begin, end = bounds - counts, bounds - 1
    flat = rank.reshape(devices)
    rank_of = lambda s: jnp.sum(jnp.where(s[:, None] == slot[None, :], flat[None, :], 0), axis=1)
    upcoming = next_map.reshape(planes, GROUP)
    same = upcoming[:, :, None] == upcoming[:, None, :]
    again = jnp.any(same & earlier[None], axis=2)
    place = jnp.sum((~again[:, None, :]) & (lane[None, :] <= lane[:, None])[None], axis=2) - 1
    where = jnp.sum(jnp.where(same & ~again[:, None, :], place[:, None, :], 0), axis=2)
    at_place = (place[:, None, :] == lane[None, :, None]) & ~again[:, None, :]
    wanted = jnp.sum(jnp.where(at_place, upcoming[:, None, :], 0), axis=2)
    table = jnp.concatenate(
        [
            cont.astype(jnp.int32).reshape(-1),
            last.reshape(-1),
            where.reshape(-1),
            wanted.reshape(-1),
            begin // GROUP,
            rank_of(begin),
            end // GROUP,
            rank_of(end),
        ]
    ).astype(jnp.int32)
    return table, jnp.max(rank) + 1, jnp.max(place) + 1


def kernel(
    planes, most_now, most_next,
    table, live, saved, cot, weights, master, moment1, moment2,
    ig_out, master_out, moment1_out, moment2_out, next_out,
    saved_v, saved_t, cot_v, weights_v, master_v, moment1_v, moment2_v, ig_v, next_v,
    grad_v, sums, fresh, now_v, later_v, xy_s, xy_r, z_s, z_r, nz_s, nz_r, nxy_s, nxy_r,
    load_sem, s1, r1, s2, r2, s3, r3, s4, r4,
):
    me = lax.axis_index("dev")
    plane, spot = me // GROUP, lax.rem(me, GROUP)
    devices = planes * GROUP
    experts, share, width = master_v.shape
    rows, hidden = saved_v.shape
    wide = width // CHUNKS
    f32, bf16 = jnp.float32, jnp.bfloat16

    loads = [
        pltpu.make_async_copy(a, b, load_sem.at[i])
        for i, (a, b) in enumerate(
            [
                (saved, saved_v), (cot, cot_v), (weights, weights_v),
                (master, master_v), (moment1, moment1_v), (moment2, moment2_v),
            ]
        )
    ]
    for load in loads:
        load.start()

    barrier = pltpu.get_barrier_semaphore()
    peers = [plane * GROUP + lax.rem(spot + o, GROUP) for o in range(1, GROUP)]
    peers += [lax.rem(plane + o, planes) * GROUP + spot for o in range(1, planes)]
    for peer in peers:
        pl.semaphore_signal(barrier, inc=1, device_id=(peer,), device_id_type=MESH)
    pl.semaphore_wait(barrier, len(peers))

    def exchange(src, dst, ssem, rsem, mine, count, device_of):
        def remote(c, other, slot):
            return pltpu.make_async_remote_copy(
                src_ref=src.at[c, other], dst_ref=dst.at[c, slot],
                send_sem=ssem.at[c, other], recv_sem=rsem.at[c, slot],
                device_id=(device_of(other),), device_id_type=MESH,
            )

        def own(c):
            return pltpu.make_async_copy(src.at[c, mine], dst.at[c, mine], rsem.at[c, mine])

        others = [lax.rem(mine + o, count) for o in range(1, count)]

        def send(c):
            for other in others:
                remote(c, other, mine).start()
            own(c).start()

        def arrived(c):
            for other in others:
                remote(c, other, other).wait_recv()
            own(c).wait()

        def sent(c):
            for other in others:
                remote(c, other, mine).wait_send()

        return send, arrived, sent

    in_plane = lambda s: plane * GROUP + s
    along_z = lambda p: p * GROUP + spot
    send_xy, arrived_xy, sent_xy = exchange(xy_s, xy_r, s1, r1, spot, GROUP, in_plane)
    send_z, arrived_z, sent_z = exchange(z_s, z_r, s2, r2, plane, planes, along_z)
    send_nz, arrived_nz, sent_nz = exchange(nz_s, nz_r, s3, r3, plane, planes, along_z)
    send_nxy, arrived_nxy, sent_nxy = exchange(nxy_s, nxy_r, s4, r4, spot, GROUP, in_plane)

    def columns(c):
        return pl.ds(pl.multiple_of(c * wide, wide), wide)

    live_count = live[0]
    loads[0].wait()
    step = 256
    for t in range(rows // step):
        index = lax.broadcasted_iota(jnp.int32, (step, hidden), 0) + t * step
        part = saved_v[t * step : (t + 1) * step, :].astype(f32)
        part = jnp.where(index < live_count, part, 0.0)
        saved_t[:, t * step : (t + 1) * step] = part.T.astype(bf16)

    loads[1].wait()

    @pl.loop(0, CHUNKS)
    def _(c):
        grad_v[...] = jnp.dot(saved_t[...], cot_v[:, columns(c)], preferred_element_type=f32)
        for s in range(GROUP):
            parts = [
                grad_v[(p * GROUP + s) * share : (p * GROUP + s + 1) * share, :]
                for p in range(planes)
            ]
            xy_s[c, s] = jnp.concatenate(parts, axis=0).astype(bf16)
        send_xy(c)

    loads[2].wait()

    @pl.loop(0, rows // step)
    def _(t):
        at = pl.ds(pl.multiple_of(t * step, step), step)
        index = lax.broadcasted_iota(jnp.int32, (step, hidden), 0) + t * step
        out = contract_cols(cot_v[at, :], weights_v[...])
        ig_v[at, :] = jnp.where(index < live_count, out, 0.0).astype(bf16)

    ig_store = pltpu.make_async_copy(ig_v, ig_out, load_sem.at[6])
    ig_store.start()

    @pl.loop(0, CHUNKS)
    def _(c):
        arrived_xy(c)
        for p in range(planes):
            total = jnp.zeros((share, wide), f32)
            for s in range(GROUP):
                keep = table[plane * GROUP + s].astype(f32)
                fresh_part = xy_r[c, s].astype(f32)[p * share : (p + 1) * share, :]
                total = total * keep + fresh_part
                sums[p, s] = total.astype(bf16)
            for k in range(most_now):
                z_s[c, p, k] = sums[p, table[devices + plane * GROUP + k]]
        send_z(c)

    for load in loads[3:]:
        load.wait()
    base = 4 * devices

    def scatter(c):
        arrived_nz(c)
        for p in range(planes):
            for k in range(most_next):
                later_v[p, k] = nz_r[c, p, k]
        for s in range(GROUP):
            place = table[2 * devices + plane * GROUP + s]
            parts = [later_v[p, place].astype(f32) for p in range(planes)]
            nxy_s[c, s] = jnp.concatenate(parts, axis=0).astype(bf16)
        send_nxy(c)

    @pl.loop(0, CHUNKS + 1)
    def _(c):
        @pl.when(c < CHUNKS)
        def _():
            arrived_z(c)
            cols = columns(c)
            for p in range(planes):
                for k in range(most_now):
                    now_v[p, k] = z_r[c, p, k]

            @pl.loop(0, experts)
            def _(e):
                begin = now_v[table[base + e], table[base + experts + e]]
                end = now_v[table[base + 2 * experts + e], table[base + 3 * experts + e]]
                split = (table[base + e] != table[base + 2 * experts + e]).astype(f32)
                grads = begin.astype(f32) + split * end.astype(f32)
                new, one, two = adam(
                    grads,
                    master_v[e, :, cols],
                    moment1_v[e, :, cols].astype(f32),
                    moment2_v[e, :, cols].astype(f32),
                )
                master_v[e, :, cols] = new
                moment1_v[e, :, cols] = one.astype(bf16)
                moment2_v[e, :, cols] = two.astype(bf16)
                fresh[e] = new.astype(bf16)

            for p in range(planes):
                for k in range(most_next):
                    nz_s[c, p, k] = fresh[table[3 * devices + p * GROUP + k]]
            send_nz(c)

        @pl.when(c > 0)
        def _():
            scatter(c - 1)

    stores = [
        pltpu.make_async_copy(a, b, load_sem.at[7 + i])
        for i, (a, b) in enumerate(
            [(master_v, master_out), (moment1_v, moment1_out), (moment2_v, moment2_out)]
        )
    ]
    for store in stores:
        store.start()

    @pl.loop(0, CHUNKS)
    def _(c):
        arrived_nxy(c)
        for p in range(planes):
            for s in range(0, GROUP, 2):
                pair = [
                    nxy_r[c, s + i].astype(f32)[p * share : (p + 1) * share, :] for i in range(2)
                ]
                at = (p * GROUP + s) * share
                next_v[at : at + 2 * share, columns(c)] = jnp.concatenate(pair, axis=0).astype(bf16)

    store = pltpu.make_async_copy(next_v, next_out, load_sem.at[10])
    store.start()

    @pl.loop(0, CHUNKS)
    def _(c):
        for sent in (sent_xy, sent_z, sent_nz, sent_nxy):
            sent(c)

    for done in [ig_store] + stores + [store]:
        done.wait()


def fused(most_now, most_next, number, table, live, saved, cot, weights, master, moment1, moment2):
    devices = lax.axis_size("dev")
    planes = devices // GROUP
    experts, share, width = master.shape
    rows, hidden = saved.shape
    wide = width // CHUNKS
    bf16, f32 = jnp.bfloat16, jnp.float32
    vmem = pltpu.VMEM
    dma = pltpu.SemaphoreType.DMA
    anywhere = pl.BlockSpec(memory_space=pl.ANY)
    scalars = pl.BlockSpec(memory_space=pltpu.SMEM)
    across = vmem((CHUNKS, GROUP, planes * share, wide), bf16)
    now = vmem((CHUNKS, planes, most_now, share, wide), bf16)
    later = vmem((CHUNKS, planes, most_next, share, wide), bf16)
    return pl.pallas_call(
        functools.partial(kernel, planes, most_now, most_next),
        out_shape=(
            jax.ShapeDtypeStruct((rows, hidden), bf16),
            jax.ShapeDtypeStruct(master.shape, f32),
            jax.ShapeDtypeStruct(moment1.shape, bf16),
            jax.ShapeDtypeStruct(moment2.shape, bf16),
            jax.ShapeDtypeStruct((hidden, width), bf16),
        ),
        in_specs=[scalars] * 2 + [anywhere] * 6,
        out_specs=(anywhere,) * 5,
        scratch_shapes=[
            vmem((rows, hidden), bf16),
            vmem((hidden, rows), bf16),
            vmem((rows, width), bf16),
            vmem((hidden, width), bf16),
            vmem(master.shape, f32),
            vmem(moment1.shape, bf16),
            vmem(moment2.shape, bf16),
            vmem((rows, hidden), bf16),
            vmem((hidden, width), bf16),
            vmem((hidden, wide), f32),
            vmem((planes, GROUP, share, wide), bf16),
            vmem((experts, share, wide), bf16),
            vmem((planes, most_now, share, wide), bf16),
            vmem((planes, most_next, share, wide), bf16),
            across, across, now, now, later, later, across, across,
            dma((11,)),
            dma((CHUNKS, GROUP)), dma((CHUNKS, GROUP)),
            dma((CHUNKS, planes)), dma((CHUNKS, planes)),
            dma((CHUNKS, planes)), dma((CHUNKS, planes)),
            dma((CHUNKS, GROUP)), dma((CHUNKS, GROUP)),
        ],
        compiler_params=pltpu.CompilerParams(
            collective_id=number, has_side_effects=True, vmem_limit_bytes=58 * 1024 * 1024
        ),
        cost_estimate=pl.CostEstimate(
            flops=4 * rows * hidden * width, bytes_accessed=26 << 20, transcendentals=0
        ),
        name=f"moe_step_{most_now}_{most_next}",
    )(table, live, saved, cot, weights, master, moment1, moment2)


def exchanged(saved, cotangent, weights, counts, live_rows, next_map, master, moment1, moment2):
    table, now, later = tables(counts, next_map, lax.axis_size("dev"))
    args = (table, live_rows, saved[0], cotangent[0], weights[0], master, moment1, moment2)
    few = GROUP - 1
    fits = (now <= few) & (later <= few)
    outs = lax.cond(
        fits,
        functools.partial(fused, few, few, 0),
        functools.partial(fused, GROUP, GROUP, 1),
        *args,
    )
    return (outs[0][None], outs[1], outs[2], outs[3], outs[4][None])


def solution(mesh):
    devices = mesh.shape["dev"]

    def per_device(*args):
        share, width = args[6].shape[1:]
        takes = devices % GROUP == 0 and GROUP >= MOST and share % 8 == 0
        takes = takes and width % (CHUNKS * 128) == 0 and args[0].shape[1] % 256 == 0
        return (exchanged if takes else plain)(*args)

    placed = (
        P("dev", None, None),
        P("dev", None, None),
        P("dev", None, None),
        P(),
        P("dev"),
        P(),
        P(None, "dev", None),
        P(None, "dev", None),
        P(None, "dev", None),
    )
    return jax.shard_map(
        per_device,
        mesh=mesh,
        in_specs=placed,
        out_specs=(
            P("dev", None, None),
            P(None, "dev", None),
            P(None, "dev", None),
            P(None, "dev", None),
            P("dev", None, None),
        ),
        check_vma=False,
    )
```

```python
import functools

import jax
import jax.numpy as jnp
from jax import lax
from jax.experimental import pallas as pl
from jax.experimental.pallas import tpu as pltpu
from jax.sharding import PartitionSpec as P

LEARN_RATE = 0.001
DECAY_RATE = 0.1
BETA_ONE = 0.9
BETA_TWO = 0.95
BIAS_ONE = 1.0 - 0.9**20
BIAS_TWO = 1.0 - 0.95**20
EPSILON = 1e-08
GROUP = 8
CHUNKS = 8
PLANES = 4
MOST = 8
FEW = 12
MESH = pl.DeviceIdType.MESH


def contract_rows(left, right):
    return lax.dot_general(
        left, right, (((0,), (0,)), ((), ())), preferred_element_type=jnp.float32
    )


def contract_cols(left, right):
    return lax.dot_general(
        left, right, (((1,), (1,)), ((), ())), preferred_element_type=jnp.float32
    )


def adam(grads, master, moment1, moment2):
    first = BETA_ONE * moment1 + (1.0 - BETA_ONE) * grads
    second = BETA_TWO * moment2 + (1.0 - BETA_TWO) * grads * grads
    update = first / BIAS_ONE / (jnp.sqrt(second / BIAS_TWO) + EPSILON) + DECAY_RATE * master
    return master - LEARN_RATE * update, first, second


def plain(saved, cotangent, weights, counts, live_rows, next_map, master, moment1, moment2):
    hidden_rows, cot_rows, slot_weights = saved[0], cotangent[0], weights[0]
    devices = lax.axis_size("dev")
    expert_count, share_rows, model_width = master.shape
    row_index = jnp.arange(hidden_rows.shape[0], dtype=jnp.int32)
    masked = jnp.where((row_index < live_rows[0])[:, None], cot_rows, jnp.zeros_like(cot_rows))
    input_grads = contract_cols(masked, slot_weights).astype(jnp.bfloat16)
    slot_grads = contract_rows(hidden_rows, masked).astype(jnp.bfloat16)
    slot_index = jnp.arange(devices, dtype=jnp.int32)
    bounds = jnp.cumsum(counts)
    holders = jnp.sum((bounds[None, :] <= slot_index[:, None]).astype(jnp.int32), axis=1)
    selector = (jnp.arange(expert_count, dtype=jnp.int32)[:, None] == holders[None, :]).astype(
        jnp.bfloat16
    )
    received = lax.all_to_all(slot_grads, "dev", split_axis=0, concat_axis=0, tiled=True)
    pieces = received.reshape(devices, share_rows, model_width)
    expert_grads = jnp.einsum("es,src->erc", selector, pieces, preferred_element_type=jnp.float32)
    master_out, first, second = adam(
        expert_grads, master, moment1.astype(jnp.float32), moment2.astype(jnp.float32)
    )
    outgoing = jnp.take(master_out.astype(jnp.bfloat16), next_map, axis=0)
    outgoing = outgoing.reshape(devices * share_rows, model_width)
    arriving = lax.all_to_all(outgoing, "dev", split_axis=0, concat_axis=0, tiled=True)
    return (
        input_grads[None],
        master_out,
        first.astype(jnp.bfloat16),
        second.astype(jnp.bfloat16),
        arriving[None],
    )


def tables(counts, next_map, devices):
    experts = counts.shape[0]
    slot = jnp.arange(devices, dtype=jnp.int32)
    ids = jnp.arange(experts, dtype=jnp.int32)
    upto = ids[None, :] <= ids[:, None]
    bounds = jnp.sum(jnp.where(upto, counts[None, :], 0), axis=1)
    holders = jnp.sum((bounds[None, :] <= slot[:, None]).astype(jnp.int32), axis=1)
    half = devices // 2
    upcoming = next_map.reshape(2, 1, half)
    present = jnp.max((upcoming == ids[None, :, None]).astype(jnp.int32), axis=2)
    place = jnp.sum(jnp.where(upto[None], present[:, None, :], 0), axis=2) - 1
    at = (place[:, None, :] == jnp.arange(half, dtype=jnp.int32)[None, :, None]) & (
        present[:, None, :] > 0
    )
    union = jnp.sum(jnp.where(at, ids[None, None, :], 0), axis=2)
    table = jnp.concatenate(
        [bounds, holders, next_map, place.reshape(-1), union.reshape(-1)]
    ).astype(jnp.int32)
    held = jnp.maximum(holders[half - 1] - holders[0], holders[devices - 1] - holders[half])
    return table, jnp.maximum(held, jnp.maximum(place[0, -1], place[1, -1])) + 1


def kernel(
    most,
    table, live, saved, cot, weights, master, moment1, moment2,
    ig_out, master_out, moment1_out, moment2_out, next_out,
    saved_v, saved_t, cot_v, weights_v, master_v, moment1_v, moment2_v, ig_v, next_v,
    grad_v, sums, fresh, own_v, half_v, mate_v, cross_v, union_v, gather_v,
    xy_s, xy_r, half_s, half_r, mate_s, mate_r, cross_s, cross_r,
    union_s, union_r, back_s, back_r, pass_s, pass_r, nxy_s, nxy_r,
    load_sem, s1, r1, s2, r2, s4, r4,
):
    me = lax.axis_index("dev")
    plane, spot = me // GROUP, lax.rem(me, GROUP)
    planes, devices = PLANES, PLANES * GROUP
    side = plane // 2
    inner = 1 + side
    is_inner = plane == inner
    mate = 2 * side + 1 - lax.rem(plane, 2)
    far = 1 - side
    far_inner, far_outer = 2 - side, 3 - 3 * side
    at_mate, at_far_inner, at_far_outer = (
        p * GROUP + spot for p in (mate, far_inner, far_outer)
    )
    experts, share, width = master_v.shape
    rows, hidden = saved_v.shape
    wide = width // CHUNKS
    f32, bf16 = jnp.float32, jnp.bfloat16

    loads = [
        pltpu.make_async_copy(a, b, load_sem.at[i])
        for i, (a, b) in enumerate(
            [
                (saved, saved_v), (cot, cot_v), (weights, weights_v),
                (master, master_v), (moment1, moment1_v), (moment2, moment2_v),
            ]
        )
    ]
    for load in loads:
        load.start()

    barrier = pltpu.get_barrier_semaphore()
    peers = [plane * GROUP + lax.rem(spot + o, GROUP) for o in range(1, GROUP)]
    peers += [lax.rem(plane + o, planes) * GROUP + spot for o in range(1, planes)]
    for peer in peers:
        pl.semaphore_signal(barrier, inc=1, device_id=(peer,), device_id_type=MESH)
    pl.semaphore_wait(barrier, len(peers))

    def exchange(src, dst, ssem, rsem, mine, count, device_of):
        def remote(c, other, slot):
            return pltpu.make_async_remote_copy(
                src_ref=src.at[c, other], dst_ref=dst.at[c, slot],
                send_sem=ssem.at[c, other], recv_sem=rsem.at[c, slot],
                device_id=(device_of(other),), device_id_type=MESH,
            )

        def own(c):
            return pltpu.make_async_copy(src.at[c, mine], dst.at[c, mine], rsem.at[c, mine])

        others = [lax.rem(mine + o, count) for o in range(1, count)]

        def send(c):
            for other in others:
                remote(c, other, mine).start()
            own(c).start()

        def arrived(c):
            for other in others:
                remote(c, other, other).wait_recv()
            own(c).wait()

        def sent(c):
            for other in others:
                remote(c, other, mine).wait_send()

        return send, arrived, sent

    in_plane = lambda s: plane * GROUP + s
    send_xy, arrived_xy, sent_xy = exchange(xy_s, xy_r, s1, r1, spot, GROUP, in_plane)
    send_nxy, arrived_nxy, sent_nxy = exchange(nxy_s, nxy_r, s4, r4, spot, GROUP, in_plane)

    def along(c, number, src, dst, device):
        return pltpu.make_async_remote_copy(
            src_ref=src, dst_ref=dst, send_sem=s2.at[c, number], recv_sem=r2.at[c, number],
            device_id=(device,), device_id_type=MESH,
        )

    def to_mate(c):
        return along(c, 0, mate_s.at[c], mate_r.at[c], at_mate)

    def half_to_mate(c):
        return along(c, 1, half_s.at[c], half_r.at[c], at_mate)

    def across_inner(c):
        return along(c, 2, cross_s.at[c, 0], cross_r.at[c], at_far_inner)

    def across_outer(c):
        return pltpu.make_async_remote_copy(
            src_ref=cross_s.at[c, 1], dst_ref=cross_r.at[c],
            send_sem=s2.at[c, 3], recv_sem=r2.at[c, 2],
            device_id=(at_far_outer,), device_id_type=MESH,
        )

    def union_to_far(c, slot):
        return pltpu.make_async_remote_copy(
            src_ref=union_s.at[c], dst_ref=union_r.at[c, slot],
            send_sem=s2.at[c, 4], recv_sem=r2.at[c, 3 + slot],
            device_id=(at_far_inner,), device_id_type=MESH,
        )

    def back_to_mate(c):
        return along(c, 5, back_s.at[c], back_r.at[c], at_mate)

    def pass_to_mate(c):
        return along(c, 6, pass_s.at[c], pass_r.at[c], at_mate)

    parity = lax.rem(plane, 2)

    def columns(c):
        return pl.ds(pl.multiple_of(c * wide, wide), wide)

    live_count = live[0]
    loads[0].wait()
    step = 256
    for t in range(rows // step):
        index = lax.broadcasted_iota(jnp.int32, (step, hidden), 0) + t * step
        part = saved_v[t * step : (t + 1) * step, :].astype(f32)
        part = jnp.where(index < live_count, part, 0.0)
        saved_t[:, t * step : (t + 1) * step] = part.T.astype(bf16)

    loads[1].wait()

    @pl.loop(0, CHUNKS)
    def _(c):
        grad_v[...] = jnp.dot(saved_t[...], cot_v[:, columns(c)], preferred_element_type=f32)
        for s in range(GROUP):
            parts = [
                grad_v[(p * GROUP + s) * share : (p * GROUP + s + 1) * share, :]
                for p in range(planes)
            ]
            xy_s[c, s] = jnp.concatenate(parts, axis=0).astype(bf16)
        send_xy(c)

    loads[2].wait()

    @pl.loop(0, rows // step)
    def _(t):
        at = pl.ds(pl.multiple_of(t * step, step), step)
        index = lax.broadcasted_iota(jnp.int32, (step, hidden), 0) + t * step
        out = contract_cols(cot_v[at, :], weights_v[...])
        ig_v[at, :] = jnp.where(index < live_count, out, 0.0).astype(bf16)

    ig_store = pltpu.make_async_copy(ig_v, ig_out, load_sem.at[6])
    ig_store.start()

    holder_at, next_at = experts, experts + devices
    place_at = experts + 2 * devices
    union_at = 3 * experts + 2 * devices

    def span(first_slot, slots):
        return table[holder_at + first_slot], table[holder_at + first_slot + slots - 1]

    def taken(e, held, most_held):
        first, last = held
        here = jnp.where(e >= first, 1.0, 0.0) * jnp.where(e <= last, 1.0, 0.0)
        return jnp.clip(e - first, 0, most_held - 1), here

    held_own = span(plane * GROUP, GROUP)
    held_mate = span(mate * GROUP, GROUP)
    held_side = span(side * 2 * GROUP, 2 * GROUP)
    held_far = span(far * 2 * GROUP, 2 * GROUP)

    def combine(c):
        half_to_mate(c).wait_recv()
        for i in range(2):
            for k in range(GROUP):
                half_v[i, k] = half_r[c, i, k]

        @pl.loop(0, most)
        def _(q):
            e = held_side[0] + q
            mine, mine_here = taken(e, held_own, GROUP)
            theirs, theirs_here = taken(e, held_mate, GROUP)
            for i in range(2):
                total = half_s[c, i, mine].astype(f32) * mine_here
                total = total + half_v[i, theirs].astype(f32) * theirs_here
                cross_s[c, i, q] = total.astype(bf16)

        across_inner(c).start()
        across_outer(c).start()

    @pl.loop(0, CHUNKS + 1)
    def _(c):
        @pl.when(c < CHUNKS)
        def _():
            arrived_xy(c)
            for p in range(planes):
                total = jnp.zeros((share, wide), f32)
                for s in range(GROUP):
                    now = plane * GROUP + s
                    if s:
                        same = table[holder_at + now] == table[holder_at + now - 1]
                        total = total * jnp.where(same, 1.0, 0.0)
                    total = total + xy_r[c, s].astype(f32)[p * share : (p + 1) * share, :]
                    sums[p, s] = total.astype(bf16)
            for k in range(GROUP):
                e = jnp.minimum(held_own[0] + k, experts - 1)
                last = jnp.clip(table[e] - 1 - plane * GROUP, 0, GROUP - 1)
                half_s[c, 0, k] = sums[far_inner, last]
                half_s[c, 1, k] = sums[far_outer, last]
                mate_s[c, k] = sums[mate, last]
                own_v[c, k] = sums[plane, last]

            @pl.when(jnp.logical_not(is_inner))
            def _():
                half_to_mate(c).start()

            to_mate(c).start()

        @pl.when((c > 0) & is_inner)
        def _():
            combine(c - 1)

    for load in loads[3:]:
        load.wait()

    def update(c):
        to_mate(c).wait_recv()
        across_inner(c).wait_recv()
        for k in range(GROUP):
            mate_v[k] = mate_r[c, k]
        for k in range(most):
            cross_v[k] = cross_r[c, k]
        cols = columns(c)

        @pl.loop(0, experts)
        def _(e):
            at_own, own_here = taken(e, held_own, GROUP)
            at_next, next_here = taken(e, held_mate, GROUP)
            at_far, far_here = taken(e, held_far, most)
            grads = own_v[c, at_own].astype(f32) * own_here
            grads = grads + mate_v[at_next].astype(f32) * next_here
            grads = grads + cross_v[at_far].astype(f32) * far_here
            new, one, two = adam(
                grads,
                master_v[e, :, cols],
                moment1_v[e, :, cols].astype(f32),
                moment2_v[e, :, cols].astype(f32),
            )
            master_v[e, :, cols] = new
            moment1_v[e, :, cols] = one.astype(bf16)
            moment2_v[e, :, cols] = two.astype(bf16)
            fresh[c, e] = new.astype(bf16)

        for q in range(most):
            union_s[c, q] = fresh[c, table[union_at + far * (devices // 2) + q]]
        union_to_far(c, parity).start()
        for s in range(GROUP):
            back_s[c, s] = fresh[c, table[next_at + mate * GROUP + s]]
        back_to_mate(c).start()

    def hand_on(c):
        for i in range(2):
            union_to_far(c, i).wait_recv()
        for i in range(2):
            for q in range(most):
                union_v[i, q] = union_r[c, i, q]
        for s in range(GROUP):
            place = table[place_at + side * experts + table[next_at + mate * GROUP + s]]
            for i in range(2):
                pass_s[c, i, s] = union_v[i, place]
        pass_to_mate(c).start()
        for s in range(GROUP):
            place = table[place_at + side * experts + table[next_at + plane * GROUP + s]]
            for i in range(2):
                gather_v[2 * far + i, s] = union_v[i, place]

    def scatter(c):
        back_to_mate(c).wait_recv()
        for s in range(GROUP):
            gather_v[plane, s] = fresh[c, table[next_at + plane * GROUP + s]]
            gather_v[mate, s] = back_r[c, s]
        for s in range(GROUP):
            parts = [gather_v[p, s].astype(f32) for p in range(planes)]
            nxy_s[c, s] = jnp.concatenate(parts, axis=0).astype(bf16)
        send_nxy(c)

    @pl.loop(0, CHUNKS + 2)
    def _(c):
        @pl.when(c < CHUNKS)
        def _():
            update(c)

        @pl.when((c > 0) & (c <= CHUNKS) & is_inner)
        def _():
            hand_on(c - 1)
            scatter(c - 1)

        @pl.when((c > 1) & jnp.logical_not(is_inner))
        def _():
            pass_to_mate(c - 2).wait_recv()
            for i in range(2):
                for s in range(GROUP):
                    gather_v[2 * far + i, s] = pass_r[c - 2, i, s]
            scatter(c - 2)

    stores = [
        pltpu.make_async_copy(a, b, load_sem.at[7 + i])
        for i, (a, b) in enumerate(
            [(master_v, master_out), (moment1_v, moment1_out), (moment2_v, moment2_out)]
        )
    ]
    for store in stores:
        store.start()

    @pl.loop(0, CHUNKS)
    def _(c):
        arrived_nxy(c)
        for p in range(planes):
            for s in range(0, GROUP, 2):
                pair = [
                    nxy_r[c, s + i].astype(f32)[p * share : (p + 1) * share, :] for i in range(2)
                ]
                at = (p * GROUP + s) * share
                next_v[at : at + 2 * share, columns(c)] = jnp.concatenate(pair, axis=0).astype(bf16)

    store = pltpu.make_async_copy(next_v, next_out, load_sem.at[10])
    store.start()

    @pl.loop(0, CHUNKS)
    def _(c):
        sent_xy(c)
        to_mate(c).wait_send()
        union_to_far(c, parity).wait_send()
        back_to_mate(c).wait_send()
        sent_nxy(c)

        @pl.when(is_inner)
        def _():
            across_inner(c).wait_send()
            across_outer(c).wait_send()
            pass_to_mate(c).wait_send()

        @pl.when(jnp.logical_not(is_inner))
        def _():
            half_to_mate(c).wait_send()

    for done in [ig_store] + stores + [store]:
        done.wait()


def fused(most, number, table, live, saved, cot, weights, master, moment1, moment2):
    experts, share, width = master.shape
    rows, hidden = saved.shape
    wide = width // CHUNKS
    bf16, f32 = jnp.bfloat16, jnp.float32
    vmem = pltpu.VMEM
    dma = pltpu.SemaphoreType.DMA
    anywhere = pl.BlockSpec(memory_space=pl.ANY)
    scalars = pl.BlockSpec(memory_space=pltpu.SMEM)
    across = vmem((CHUNKS, GROUP, PLANES * share, wide), bf16)
    blocks = lambda *lead: vmem((*lead, share, wide), bf16)
    return pl.pallas_call(
        functools.partial(kernel, most),
        out_shape=(
            jax.ShapeDtypeStruct((rows, hidden), bf16),
            jax.ShapeDtypeStruct(master.shape, f32),
            jax.ShapeDtypeStruct(moment1.shape, bf16),
            jax.ShapeDtypeStruct(moment2.shape, bf16),
            jax.ShapeDtypeStruct((hidden, width), bf16),
        ),
        in_specs=[scalars] * 2 + [anywhere] * 6,
        out_specs=(anywhere,) * 5,
        scratch_shapes=[
            vmem((rows, hidden), bf16),
            vmem((hidden, rows), bf16),
            vmem((rows, width), bf16),
            vmem((hidden, width), bf16),
            vmem(master.shape, f32),
            vmem(moment1.shape, bf16),
            vmem(moment2.shape, bf16),
            vmem((rows, hidden), bf16),
            vmem((hidden, width), bf16),
            vmem((hidden, wide), f32),
            blocks(PLANES, GROUP),
            blocks(CHUNKS, experts),
            blocks(CHUNKS, GROUP), blocks(2, GROUP), blocks(GROUP),
            blocks(most), blocks(2, most), blocks(PLANES, GROUP),
            across, across,
            blocks(CHUNKS, 2, GROUP), blocks(CHUNKS, 2, GROUP),
            blocks(CHUNKS, GROUP), blocks(CHUNKS, GROUP),
            blocks(CHUNKS, 2, most), blocks(CHUNKS, most),
            blocks(CHUNKS, most), blocks(CHUNKS, 2, most),
            blocks(CHUNKS, GROUP), blocks(CHUNKS, GROUP),
            blocks(CHUNKS, 2, GROUP), blocks(CHUNKS, 2, GROUP),
            across, across,
            dma((11,)),
            dma((CHUNKS, GROUP)), dma((CHUNKS, GROUP)),
            dma((CHUNKS, 7)), dma((CHUNKS, 7)),
            dma((CHUNKS, GROUP)), dma((CHUNKS, GROUP)),
        ],
        compiler_params=pltpu.CompilerParams(
            collective_id=number, has_side_effects=True, vmem_limit_bytes=58 * 1024 * 1024
        ),
        cost_estimate=pl.CostEstimate(
            flops=4 * rows * hidden * width, bytes_accessed=26 << 20, transcendentals=0
        ),
        name=f"moe_step_{most}",
    )(table, live, saved, cot, weights, master, moment1, moment2)


def exchanged(saved, cotangent, weights, counts, live_rows, next_map, master, moment1, moment2):
    devices = lax.axis_size("dev")
    table, distinct = tables(counts, next_map, devices)
    args = (table, live_rows, saved[0], cotangent[0], weights[0], master, moment1, moment2)
    outs = lax.cond(
        distinct <= FEW,
        functools.partial(fused, FEW, 0),
        functools.partial(fused, devices // 2, 1),
        *args,
    )
    return (outs[0][None], outs[1], outs[2], outs[3], outs[4][None])


def solution(mesh):
    devices = mesh.shape["dev"]

    def per_device(*args):
        share, width = args[6].shape[1:]
        takes = devices == PLANES * GROUP and GROUP >= MOST and share % 8 == 0
        takes = takes and width % (CHUNKS * 128) == 0 and args[0].shape[1] % 256 == 0
        return (exchanged if takes else plain)(*args)

    placed = (
        P("dev", None, None),
        P("dev", None, None),
        P("dev", None, None),
        P(),
        P("dev"),
        P(),
        P(None, "dev", None),
        P(None, "dev", None),
        P(None, "dev", None),
    )
    return jax.shard_map(
        per_device,
        mesh=mesh,
        in_specs=placed,
        out_specs=(
            P("dev", None, None),
            P(None, "dev", None),
            P(None, "dev", None),
            P(None, "dev", None),
            P("dev", None, None),
        ),
        check_vma=False,
    )
```

```python
import functools

import jax
import jax.numpy as jnp
from jax import lax
from jax.experimental import pallas as pl
from jax.experimental.pallas import tpu as pltpu
from jax.sharding import PartitionSpec as P

LEARN_RATE = 0.001
DECAY_RATE = 0.1
BETA_ONE = 0.9
BETA_TWO = 0.95
BIAS_ONE = 1.0 - 0.9**20
BIAS_TWO = 1.0 - 0.95**20
EPSILON = 1e-08
GROUP = 8
CHUNKS = 8
PLANES = 4
MOST = 8
FEW = 12
MESH = pl.DeviceIdType.MESH


def contract_rows(left, right):
    return lax.dot_general(
        left, right, (((0,), (0,)), ((), ())), preferred_element_type=jnp.float32
    )


def contract_cols(left, right):
    return lax.dot_general(
        left, right, (((1,), (1,)), ((), ())), preferred_element_type=jnp.float32
    )


def adam(grads, master, moment1, moment2):
    first = BETA_ONE * moment1 + (1.0 - BETA_ONE) * grads
    second = BETA_TWO * moment2 + (1.0 - BETA_TWO) * grads * grads
    update = first / BIAS_ONE / (jnp.sqrt(second / BIAS_TWO) + EPSILON) + DECAY_RATE * master
    return master - LEARN_RATE * update, first, second


def plain(saved, cotangent, weights, counts, live_rows, next_map, master, moment1, moment2):
    hidden_rows, cot_rows, slot_weights = saved[0], cotangent[0], weights[0]
    devices = lax.axis_size("dev")
    expert_count, share_rows, model_width = master.shape
    row_index = jnp.arange(hidden_rows.shape[0], dtype=jnp.int32)
    masked = jnp.where((row_index < live_rows[0])[:, None], cot_rows, jnp.zeros_like(cot_rows))
    input_grads = contract_cols(masked, slot_weights).astype(jnp.bfloat16)
    slot_grads = contract_rows(hidden_rows, masked).astype(jnp.bfloat16)
    slot_index = jnp.arange(devices, dtype=jnp.int32)
    bounds = jnp.cumsum(counts)
    holders = jnp.sum((bounds[None, :] <= slot_index[:, None]).astype(jnp.int32), axis=1)
    selector = (jnp.arange(expert_count, dtype=jnp.int32)[:, None] == holders[None, :]).astype(
        jnp.bfloat16
    )
    received = lax.all_to_all(slot_grads, "dev", split_axis=0, concat_axis=0, tiled=True)
    pieces = received.reshape(devices, share_rows, model_width)
    expert_grads = jnp.einsum("es,src->erc", selector, pieces, preferred_element_type=jnp.float32)
    master_out, first, second = adam(
        expert_grads, master, moment1.astype(jnp.float32), moment2.astype(jnp.float32)
    )
    outgoing = jnp.take(master_out.astype(jnp.bfloat16), next_map, axis=0)
    outgoing = outgoing.reshape(devices * share_rows, model_width)
    arriving = lax.all_to_all(outgoing, "dev", split_axis=0, concat_axis=0, tiled=True)
    return (
        input_grads[None],
        master_out,
        first.astype(jnp.bfloat16),
        second.astype(jnp.bfloat16),
        arriving[None],
    )


def plan(counts, next_map, table, distinct):
    experts, devices = counts.shape[0], next_map.shape[0]
    half = devices // 2
    holder_at, next_at = experts, experts + devices
    place_at = experts + 2 * devices
    union_at = place_at + 2 * experts

    def bound(e, total):
        table[e] = total + counts[e]
        return total + counts[e]

    lax.fori_loop(0, experts, bound, jnp.int32(0))

    def clear(i, _):
        table[place_at + i] = 0
        return _

    lax.fori_loop(0, 2 * experts + devices, clear, jnp.int32(0))

    def holder(s, e):
        e = jnp.minimum(jnp.where(table[e] <= s, e + 1, e), experts - 1)
        table[holder_at + s] = e
        e_next = next_map[s]
        table[next_at + s] = e_next
        table[place_at + (s // half) * experts + e_next] = 1
        return e

    lax.fori_loop(0, devices, holder, jnp.int32(0))
    most = jnp.maximum(
        table[holder_at + half - 1] - table[holder_at],
        table[holder_at + devices - 1] - table[holder_at + half],
    )
    most = most + 1
    for h in range(2):

        def rank(e, held, h=h):
            here = table[place_at + h * experts + e]
            table[place_at + h * experts + e] = held

            @pl.when(here == 1)
            def _():
                table[union_at + h * half + held] = e

            return held + here

        most = jnp.maximum(most, lax.fori_loop(0, experts, rank, jnp.int32(0)))
    distinct[0] = most


def tables(counts, next_map):
    experts, devices = counts.shape[0], next_map.shape[0]
    scalars = pl.BlockSpec(memory_space=pltpu.SMEM)
    return pl.pallas_call(
        plan,
        out_shape=(
            jax.ShapeDtypeStruct((3 * experts + 3 * devices,), jnp.int32),
            jax.ShapeDtypeStruct((1,), jnp.int32),
        ),
        in_specs=[scalars] * 2,
        out_specs=(scalars,) * 2,
        name="plan",
    )(counts, next_map)


def kernel(
    most,
    table, live, saved, cot, weights, master, moment1, moment2,
    ig_out, master_out, moment1_out, moment2_out, next_out,
    saved_v, saved_t, cot_v, weights_v, master_v, moment1_v, moment2_v, ig_v, next_v,
    grad_v, sums, fresh, own_v, half_v, mate_v, cross_v, union_v, gather_v,
    xy_s, xy_r, half_s, half_r, mate_s, mate_r, cross_s, cross_r,
    union_s, union_r, back_s, back_r, pass_s, pass_r, nxy_s, nxy_r,
    load_sem, s1, r1, s2, r2, s4, r4,
):
    me = lax.axis_index("dev")
    plane, spot = me // GROUP, lax.rem(me, GROUP)
    planes, devices = PLANES, PLANES * GROUP
    side = plane // 2
    inner = 1 + side
    is_inner = plane == inner
    mate = 2 * side + 1 - lax.rem(plane, 2)
    far = 1 - side
    far_inner, far_outer = 2 - side, 3 - 3 * side
    at_mate, at_far_inner, at_far_outer = (
        p * GROUP + spot for p in (mate, far_inner, far_outer)
    )
    experts, share, width = master_v.shape
    rows, hidden = saved_v.shape
    wide = width // CHUNKS
    f32, bf16 = jnp.float32, jnp.bfloat16

    loads = [
        pltpu.make_async_copy(a, b, load_sem.at[i])
        for i, (a, b) in enumerate(
            [
                (saved, saved_v), (cot, cot_v), (weights, weights_v),
                (master, master_v), (moment1, moment1_v), (moment2, moment2_v),
            ]
        )
    ]
    for load in loads:
        load.start()

    barrier = pltpu.get_barrier_semaphore()
    peers = [plane * GROUP + lax.rem(spot + o, GROUP) for o in range(1, GROUP)]
    peers += [lax.rem(plane + o, planes) * GROUP + spot for o in range(1, planes)]
    for peer in peers:
        pl.semaphore_signal(barrier, inc=1, device_id=(peer,), device_id_type=MESH)
    pl.semaphore_wait(barrier, len(peers))

    def exchange(src, dst, ssem, rsem, mine, count, device_of):
        def remote(c, other, slot):
            return pltpu.make_async_remote_copy(
                src_ref=src.at[c, other], dst_ref=dst.at[c, slot],
                send_sem=ssem.at[c, other], recv_sem=rsem.at[c, slot],
                device_id=(device_of(other),), device_id_type=MESH,
            )

        def own(c):
            return pltpu.make_async_copy(src.at[c, mine], dst.at[c, mine], rsem.at[c, mine])

        others = [lax.rem(mine + o, count) for o in range(1, count)]

        def send(c):
            for other in others:
                remote(c, other, mine).start()
            own(c).start()

        def arrived(c):
            for other in others:
                remote(c, other, other).wait_recv()
            own(c).wait()

        def sent(c):
            for other in others:
                remote(c, other, mine).wait_send()

        return send, arrived, sent

    in_plane = lambda s: plane * GROUP + s
    send_xy, arrived_xy, sent_xy = exchange(xy_s, xy_r, s1, r1, spot, GROUP, in_plane)
    send_nxy, arrived_nxy, sent_nxy = exchange(nxy_s, nxy_r, s4, r4, spot, GROUP, in_plane)

    def along(c, number, src, dst, device):
        return pltpu.make_async_remote_copy(
            src_ref=src, dst_ref=dst, send_sem=s2.at[c, number], recv_sem=r2.at[c, number],
            device_id=(device,), device_id_type=MESH,
        )

    def to_mate(c):
        return along(c, 0, mate_s.at[c], mate_r.at[c], at_mate)

    def half_to_mate(c):
        return along(c, 1, half_s.at[c], half_r.at[c], at_mate)

    def across_inner(c):
        return along(c, 2, cross_s.at[c, 0], cross_r.at[c], at_far_inner)

    def across_outer(c):
        return pltpu.make_async_remote_copy(
            src_ref=cross_s.at[c, 1], dst_ref=cross_r.at[c],
            send_sem=s2.at[c, 3], recv_sem=r2.at[c, 2],
            device_id=(at_far_outer,), device_id_type=MESH,
        )

    def union_to_far(c, slot):
        return pltpu.make_async_remote_copy(
            src_ref=union_s.at[c], dst_ref=union_r.at[c, slot],
            send_sem=s2.at[c, 4], recv_sem=r2.at[c, 3 + slot],
            device_id=(at_far_inner,), device_id_type=MESH,
        )

    def back_to_mate(c):
        return along(c, 5, back_s.at[c], back_r.at[c], at_mate)

    def pass_to_mate(c):
        return along(c, 6, pass_s.at[c], pass_r.at[c], at_mate)

    parity = lax.rem(plane, 2)

    def columns(c):
        return pl.ds(pl.multiple_of(c * wide, wide), wide)

    live_count = live[0]
    loads[0].wait()
    step = rows // 4
    for t in range(rows // step):
        index = lax.broadcasted_iota(jnp.int32, (step, hidden), 0) + t * step
        part = saved_v[t * step : (t + 1) * step, :].astype(f32)
        part = jnp.where(index < live_count, part, 0.0)
        saved_t[:, t * step : (t + 1) * step] = part.T.astype(bf16)

    loads[1].wait()

    def multiply(c):
        grad_v[...] = jnp.dot(saved_t[...], cot_v[:, columns(c)], preferred_element_type=f32)
        for s in range(GROUP):
            parts = [
                grad_v[(p * GROUP + s) * share : (p * GROUP + s + 1) * share, :]
                for p in range(planes)
            ]
            xy_s[c, s] = jnp.concatenate(parts, axis=0).astype(bf16)
        send_xy(c)

    def turn_back(t):
        few = rows // CHUNKS
        at = pl.ds(pl.multiple_of(t * few, few), few)
        index = lax.broadcasted_iota(jnp.int32, (few, hidden), 0) + t * few
        out = contract_cols(cot_v[at, :], weights_v[...])
        ig_v[at, :] = jnp.where(index < live_count, out, 0.0).astype(bf16)

    holder_at, next_at = experts, experts + devices
    place_at = experts + 2 * devices
    union_at = 3 * experts + 2 * devices

    def span(first_slot, slots):
        return table[holder_at + first_slot], table[holder_at + first_slot + slots - 1]

    def taken(e, held, most_held):
        first, last = held
        here = jnp.where(e >= first, 1.0, 0.0) * jnp.where(e <= last, 1.0, 0.0)
        return jnp.clip(e - first, 0, most_held - 1), here

    held_own = span(plane * GROUP, GROUP)
    held_mate = span(mate * GROUP, GROUP)
    held_side = span(side * 2 * GROUP, 2 * GROUP)
    held_far = span(far * 2 * GROUP, 2 * GROUP)

    def combine(c):
        half_to_mate(c).wait_recv()
        for i in range(2):
            for k in range(GROUP):
                half_v[i, k] = half_r[c, i, k]

        @pl.loop(0, most)
        def _(q):
            e = held_side[0] + q
            mine, mine_here = taken(e, held_own, GROUP)
            theirs, theirs_here = taken(e, held_mate, GROUP)
            for i in range(2):
                total = half_s[c, i, mine].astype(f32) * mine_here
                total = total + half_v[i, theirs].astype(f32) * theirs_here
                cross_s[c, i, q] = total.astype(bf16)

        across_inner(c).start()
        across_outer(c).start()

    def reduce(c):
        arrived_xy(c)
        for p in range(planes):
            total = jnp.zeros((share, wide), f32)
            for s in range(GROUP):
                now = plane * GROUP + s
                if s:
                    same = table[holder_at + now] == table[holder_at + now - 1]
                    total = total * jnp.where(same, 1.0, 0.0)
                total = total + xy_r[c, s].astype(f32)[p * share : (p + 1) * share, :]
                sums[p, s] = total.astype(bf16)
        for k in range(GROUP):
            e = jnp.minimum(held_own[0] + k, experts - 1)
            last = jnp.clip(table[e] - 1 - plane * GROUP, 0, GROUP - 1)
            half_s[c, 0, k] = sums[far_inner, last]
            half_s[c, 1, k] = sums[far_outer, last]
            mate_s[c, k] = sums[mate, last]
            own_v[c, k] = sums[plane, last]

        @pl.when(jnp.logical_not(is_inner))
        def _():
            half_to_mate(c).start()

        to_mate(c).start()

    for c in range(2):
        multiply(c)
    loads[2].wait()

    @pl.loop(2, CHUNKS + 3)
    def _(c):
        @pl.when(c < CHUNKS)
        def _():
            multiply(c)

        @pl.when(c < CHUNKS + 2)
        def _():
            reduce(c - 2)

        @pl.when((c > 2) & is_inner)
        def _():
            combine(c - 3)

        @pl.when(c < CHUNKS + 2)
        def _():
            turn_back(c - 2)

    ig_store = pltpu.make_async_copy(ig_v, ig_out, load_sem.at[6])
    ig_store.start()

    for load in loads[3:]:
        load.wait()

    def update(c):
        to_mate(c).wait_recv()
        across_inner(c).wait_recv()
        for k in range(GROUP):
            mate_v[k] = mate_r[c, k]
        for k in range(most):
            cross_v[k] = cross_r[c, k]
        cols = columns(c)

        @pl.loop(0, experts)
        def _(e):
            at_own, own_here = taken(e, held_own, GROUP)
            at_next, next_here = taken(e, held_mate, GROUP)
            at_far, far_here = taken(e, held_far, most)
            grads = own_v[c, at_own].astype(f32) * own_here
            grads = grads + mate_v[at_next].astype(f32) * next_here
            grads = grads + cross_v[at_far].astype(f32) * far_here
            new, one, two = adam(
                grads,
                master_v[e, :, cols],
                moment1_v[e, :, cols].astype(f32),
                moment2_v[e, :, cols].astype(f32),
            )
            master_v[e, :, cols] = new
            moment1_v[e, :, cols] = one.astype(bf16)
            moment2_v[e, :, cols] = two.astype(bf16)
            fresh[c, e] = new.astype(bf16)

        for q in range(most):
            union_s[c, q] = fresh[c, table[union_at + far * (devices // 2) + q]]
        union_to_far(c, parity).start()
        for s in range(GROUP):
            back_s[c, s] = fresh[c, table[next_at + mate * GROUP + s]]
        back_to_mate(c).start()

    def hand_on(c):
        for i in range(2):
            union_to_far(c, i).wait_recv()
        for i in range(2):
            for q in range(most):
                union_v[i, q] = union_r[c, i, q]
        for s in range(GROUP):
            place = table[place_at + side * experts + table[next_at + mate * GROUP + s]]
            for i in range(2):
                pass_s[c, i, s] = union_v[i, place]
        pass_to_mate(c).start()
        for s in range(GROUP):
            place = table[place_at + side * experts + table[next_at + plane * GROUP + s]]
            for i in range(2):
                gather_v[2 * far + i, s] = union_v[i, place]

    def scatter(c):
        back_to_mate(c).wait_recv()
        for s in range(GROUP):
            gather_v[plane, s] = fresh[c, table[next_at + plane * GROUP + s]]
            gather_v[mate, s] = back_r[c, s]
        for s in range(GROUP):
            parts = [gather_v[p, s].astype(f32) for p in range(planes)]
            nxy_s[c, s] = jnp.concatenate(parts, axis=0).astype(bf16)
        send_nxy(c)

    @pl.loop(0, CHUNKS + 2)
    def _(c):
        @pl.when(c < CHUNKS)
        def _():
            update(c)

        @pl.when((c > 0) & (c <= CHUNKS) & is_inner)
        def _():
            hand_on(c - 1)
            scatter(c - 1)

        @pl.when((c > 1) & jnp.logical_not(is_inner))
        def _():
            pass_to_mate(c - 2).wait_recv()
            for i in range(2):
                for s in range(GROUP):
                    gather_v[2 * far + i, s] = pass_r[c - 2, i, s]
            scatter(c - 2)

    stores = [
        pltpu.make_async_copy(a, b, load_sem.at[7 + i])
        for i, (a, b) in enumerate(
            [(master_v, master_out), (moment1_v, moment1_out), (moment2_v, moment2_out)]
        )
    ]
    for store in stores:
        store.start()

    @pl.loop(0, CHUNKS)
    def _(c):
        arrived_nxy(c)
        for p in range(planes):
            for s in range(0, GROUP, 2):
                pair = [
                    nxy_r[c, s + i].astype(f32)[p * share : (p + 1) * share, :] for i in range(2)
                ]
                at = (p * GROUP + s) * share
                next_v[at : at + 2 * share, columns(c)] = jnp.concatenate(pair, axis=0).astype(bf16)

    store = pltpu.make_async_copy(next_v, next_out, load_sem.at[10])
    store.start()

    @pl.loop(0, CHUNKS)
    def _(c):
        sent_xy(c)
        to_mate(c).wait_send()
        union_to_far(c, parity).wait_send()
        back_to_mate(c).wait_send()
        sent_nxy(c)

        @pl.when(is_inner)
        def _():
            across_inner(c).wait_send()
            across_outer(c).wait_send()
            pass_to_mate(c).wait_send()

        @pl.when(jnp.logical_not(is_inner))
        def _():
            half_to_mate(c).wait_send()

    for done in [ig_store] + stores + [store]:
        done.wait()


def fused(most, number, table, live, saved, cot, weights, master, moment1, moment2):
    experts, share, width = master.shape
    rows, hidden = saved.shape
    wide = width // CHUNKS
    bf16, f32 = jnp.bfloat16, jnp.float32
    vmem = pltpu.VMEM
    dma = pltpu.SemaphoreType.DMA
    anywhere = pl.BlockSpec(memory_space=pl.ANY)
    scalars = pl.BlockSpec(memory_space=pltpu.SMEM)
    across = vmem((CHUNKS, GROUP, PLANES * share, wide), bf16)
    blocks = lambda *lead: vmem((*lead, share, wide), bf16)
    return pl.pallas_call(
        functools.partial(kernel, most),
        out_shape=(
            jax.ShapeDtypeStruct((rows, hidden), bf16),
            jax.ShapeDtypeStruct(master.shape, f32),
            jax.ShapeDtypeStruct(moment1.shape, bf16),
            jax.ShapeDtypeStruct(moment2.shape, bf16),
            jax.ShapeDtypeStruct((hidden, width), bf16),
        ),
        in_specs=[scalars] * 2 + [anywhere] * 6,
        out_specs=(anywhere,) * 5,
        scratch_shapes=[
            vmem((rows, hidden), bf16),
            vmem((hidden, rows), bf16),
            vmem((rows, width), bf16),
            vmem((hidden, width), bf16),
            vmem(master.shape, f32),
            vmem(moment1.shape, bf16),
            vmem(moment2.shape, bf16),
            vmem((rows, hidden), bf16),
            vmem((hidden, width), bf16),
            vmem((hidden, wide), f32),
            blocks(PLANES, GROUP),
            blocks(CHUNKS, experts),
            blocks(CHUNKS, GROUP), blocks(2, GROUP), blocks(GROUP),
            blocks(most), blocks(2, most), blocks(PLANES, GROUP),
            across, across,
            blocks(CHUNKS, 2, GROUP), blocks(CHUNKS, 2, GROUP),
            blocks(CHUNKS, GROUP), blocks(CHUNKS, GROUP),
            blocks(CHUNKS, 2, most), blocks(CHUNKS, most),
            blocks(CHUNKS, most), blocks(CHUNKS, 2, most),
            blocks(CHUNKS, GROUP), blocks(CHUNKS, GROUP),
            blocks(CHUNKS, 2, GROUP), blocks(CHUNKS, 2, GROUP),
            across, across,
            dma((11,)),
            dma((CHUNKS, GROUP)), dma((CHUNKS, GROUP)),
            dma((CHUNKS, 7)), dma((CHUNKS, 7)),
            dma((CHUNKS, GROUP)), dma((CHUNKS, GROUP)),
        ],
        compiler_params=pltpu.CompilerParams(
            collective_id=number, has_side_effects=True, vmem_limit_bytes=58 * 1024 * 1024
        ),
        cost_estimate=pl.CostEstimate(
            flops=4 * rows * hidden * width, bytes_accessed=26 << 20, transcendentals=0
        ),
        name=f"moe_step_{most}",
    )(table, live, saved, cot, weights, master, moment1, moment2)


def exchanged(saved, cotangent, weights, counts, live_rows, next_map, master, moment1, moment2):
    devices = lax.axis_size("dev")
    table, distinct = tables(counts, next_map)
    args = (table, live_rows, saved[0], cotangent[0], weights[0], master, moment1, moment2)
    outs = lax.cond(
        distinct[0] <= FEW,
        functools.partial(fused, FEW, 0),
        functools.partial(fused, devices // 2, 1),
        *args,
    )
    return (outs[0][None], outs[1], outs[2], outs[3], outs[4][None])


def solution(mesh):
    devices = mesh.shape["dev"]

    def per_device(*args):
        share, width = args[6].shape[1:]
        takes = devices == PLANES * GROUP and GROUP >= MOST and share % 8 == 0
        takes = takes and width % (CHUNKS * 128) == 0 and args[0].shape[1] % (CHUNKS * 16) == 0
        return (exchanged if takes else plain)(*args)

    placed = (
        P("dev", None, None),
        P("dev", None, None),
        P("dev", None, None),
        P(),
        P("dev"),
        P(),
        P(None, "dev", None),
        P(None, "dev", None),
        P(None, "dev", None),
    )
    return jax.shard_map(
        per_device,
        mesh=mesh,
        in_specs=placed,
        out_specs=(
            P("dev", None, None),
            P(None, "dev", None),
            P(None, "dev", None),
            P(None, "dev", None),
            P("dev", None, None),
        ),
        check_vma=False,
    )
```

```python
import functools

import jax
import jax.numpy as jnp
from jax import lax
from jax.experimental import pallas as pl
from jax.experimental.pallas import tpu as pltpu
from jax.sharding import PartitionSpec as P

LEARN_RATE = 0.001
DECAY_RATE = 0.1
BETA_ONE = 0.9
BETA_TWO = 0.95
BIAS_ONE = 1.0 - 0.9**20
BIAS_TWO = 1.0 - 0.95**20
EPSILON = 1e-08
GROUP = 8
CHUNKS = 16
PLANES = 4
MOST = 8
FEW = 12
MESH = pl.DeviceIdType.MESH


def contract_rows(left, right):
    return lax.dot_general(
        left, right, (((0,), (0,)), ((), ())), preferred_element_type=jnp.float32
    )


def contract_cols(left, right):
    return lax.dot_general(
        left, right, (((1,), (1,)), ((), ())), preferred_element_type=jnp.float32
    )


def adam(grads, master, moment1, moment2):
    first = BETA_ONE * moment1 + (1.0 - BETA_ONE) * grads
    second = BETA_TWO * moment2 + (1.0 - BETA_TWO) * grads * grads
    update = first / BIAS_ONE / (jnp.sqrt(second / BIAS_TWO) + EPSILON) + DECAY_RATE * master
    return master - LEARN_RATE * update, first, second


def plain(saved, cotangent, weights, counts, live_rows, next_map, master, moment1, moment2):
    hidden_rows, cot_rows, slot_weights = saved[0], cotangent[0], weights[0]
    devices = lax.axis_size("dev")
    expert_count, share_rows, model_width = master.shape
    row_index = jnp.arange(hidden_rows.shape[0], dtype=jnp.int32)
    masked = jnp.where((row_index < live_rows[0])[:, None], cot_rows, jnp.zeros_like(cot_rows))
    input_grads = contract_cols(masked, slot_weights).astype(jnp.bfloat16)
    slot_grads = contract_rows(hidden_rows, masked).astype(jnp.bfloat16)
    slot_index = jnp.arange(devices, dtype=jnp.int32)
    bounds = jnp.cumsum(counts)
    holders = jnp.sum((bounds[None, :] <= slot_index[:, None]).astype(jnp.int32), axis=1)
    selector = (jnp.arange(expert_count, dtype=jnp.int32)[:, None] == holders[None, :]).astype(
        jnp.bfloat16
    )
    received = lax.all_to_all(slot_grads, "dev", split_axis=0, concat_axis=0, tiled=True)
    pieces = received.reshape(devices, share_rows, model_width)
    expert_grads = jnp.einsum("es,src->erc", selector, pieces, preferred_element_type=jnp.float32)
    master_out, first, second = adam(
        expert_grads, master, moment1.astype(jnp.float32), moment2.astype(jnp.float32)
    )
    outgoing = jnp.take(master_out.astype(jnp.bfloat16), next_map, axis=0)
    outgoing = outgoing.reshape(devices * share_rows, model_width)
    arriving = lax.all_to_all(outgoing, "dev", split_axis=0, concat_axis=0, tiled=True)
    return (
        input_grads[None],
        master_out,
        first.astype(jnp.bfloat16),
        second.astype(jnp.bfloat16),
        arriving[None],
    )


def plan(counts, next_map, table, distinct):
    experts, devices = counts.shape[0], next_map.shape[0]
    half = devices // 2
    holder_at, next_at = experts, experts + devices
    place_at = experts + 2 * devices
    union_at = place_at + 2 * experts

    def bound(e, total):
        table[e] = total + counts[e]
        return total + counts[e]

    lax.fori_loop(0, experts, bound, jnp.int32(0))

    def clear(i, _):
        table[place_at + i] = 0
        return _

    lax.fori_loop(0, 2 * experts + devices, clear, jnp.int32(0))

    def holder(s, e):
        e = jnp.minimum(jnp.where(table[e] <= s, e + 1, e), experts - 1)
        table[holder_at + s] = e
        e_next = next_map[s]
        table[next_at + s] = e_next
        table[place_at + (s // half) * experts + e_next] = 1
        return e

    lax.fori_loop(0, devices, holder, jnp.int32(0))
    most = jnp.maximum(
        table[holder_at + half - 1] - table[holder_at],
        table[holder_at + devices - 1] - table[holder_at + half],
    )
    most = most + 1
    for h in range(2):

        def rank(e, held, h=h):
            here = table[place_at + h * experts + e]
            table[place_at + h * experts + e] = held

            @pl.when(here == 1)
            def _():
                table[union_at + h * half + held] = e

            return held + here

        most = jnp.maximum(most, lax.fori_loop(0, experts, rank, jnp.int32(0)))
    distinct[0] = most


def tables(counts, next_map):
    experts, devices = counts.shape[0], next_map.shape[0]
    scalars = pl.BlockSpec(memory_space=pltpu.SMEM)
    return pl.pallas_call(
        plan,
        out_shape=(
            jax.ShapeDtypeStruct((3 * experts + 3 * devices,), jnp.int32),
            jax.ShapeDtypeStruct((1,), jnp.int32),
        ),
        in_specs=[scalars] * 2,
        out_specs=(scalars,) * 2,
        name="plan",
    )(counts, next_map)


def kernel(
    most,
    table, live, saved, cot, weights, master, moment1, moment2,
    ig_out, master_out, moment1_out, moment2_out, next_out,
    saved_v, saved_t, cot_v, weights_v, master_v, moment1_v, moment2_v,
    grad_v, sums, fresh, own_v, half_v, mate_v, cross_v, union_v, gather_v,
    xy_s, xy_r, half_s, half_r, mate_s, mate_r, cross_s, cross_r,
    union_s, union_r, back_s, back_r, pass_s, pass_r, nxy_r,
    load_sem, s1, r1, s2, r2, s4, r4, s5,
):
    me = lax.axis_index("dev")
    plane, spot = me // GROUP, lax.rem(me, GROUP)
    planes, devices = PLANES, PLANES * GROUP
    ig_v, next_v, nxy_s = saved_v, weights_v, xy_s
    side = plane // 2
    inner = 1 + side
    is_inner = plane == inner
    mate = 2 * side + 1 - lax.rem(plane, 2)
    far = 1 - side
    far_inner, far_outer = 2 - side, 3 - 3 * side
    at_mate, at_far_inner, at_far_outer = (
        p * GROUP + spot for p in (mate, far_inner, far_outer)
    )
    experts, share, width = master_v.shape
    rows, hidden = saved_v.shape
    wide = width // CHUNKS
    f32, bf16 = jnp.float32, jnp.bfloat16

    loads = [
        pltpu.make_async_copy(a, b, load_sem.at[i])
        for i, (a, b) in enumerate(
            [
                (saved, saved_v), (cot, cot_v), (weights, weights_v),
                (master, master_v), (moment1, moment1_v), (moment2, moment2_v),
            ]
        )
    ]
    for load in loads:
        load.start()

    barrier = pltpu.get_barrier_semaphore()
    peers = [plane * GROUP + lax.rem(spot + o, GROUP) for o in range(1, GROUP)]
    peers += [lax.rem(plane + o, planes) * GROUP + spot for o in range(1, planes)]
    for peer in peers:
        pl.semaphore_signal(barrier, inc=1, device_id=(peer,), device_id_type=MESH)
    pl.semaphore_wait(barrier, len(peers))

    def exchange(src, dst, ssem, rsem, mine, count, device_of):
        def remote(c, other, slot):
            return pltpu.make_async_remote_copy(
                src_ref=src.at[c, other], dst_ref=dst.at[c, slot],
                send_sem=ssem.at[c, other], recv_sem=rsem.at[c, slot],
                device_id=(device_of(other),), device_id_type=MESH,
            )

        def own(c):
            return pltpu.make_async_copy(src.at[c, mine], dst.at[c, mine], rsem.at[c, mine])

        others = [lax.rem(mine + o, count) for o in range(1, count)]

        def send(c):
            for other in others:
                remote(c, other, mine).start()
            own(c).start()

        def arrived(c):
            for other in others:
                remote(c, other, other).wait_recv()
            own(c).wait()

        def sent(c):
            for other in others:
                remote(c, other, mine).wait_send()

        return send, arrived, sent

    in_plane = lambda s: plane * GROUP + s
    send_xy, arrived_xy, sent_xy = exchange(xy_s, xy_r, s1, r1, spot, GROUP, in_plane)
    send_nxy, arrived_nxy, sent_nxy = exchange(nxy_s, nxy_r, s4, r4, spot, GROUP, in_plane)

    def along(c, number, src, dst, device):
        return pltpu.make_async_remote_copy(
            src_ref=src, dst_ref=dst, send_sem=s2.at[c, number], recv_sem=r2.at[c, number],
            device_id=(device,), device_id_type=MESH,
        )

    def to_mate(c):
        return along(c, 0, mate_s.at[c], mate_r.at[c], at_mate)

    def half_to_mate(c):
        return along(c, 1, half_s.at[c], half_r.at[c], at_mate)

    def across_inner(c):
        return along(c, 2, cross_s.at[c, 0], cross_r.at[c], at_far_inner)

    def across_outer(c):
        return pltpu.make_async_remote_copy(
            src_ref=cross_s.at[c, 1], dst_ref=cross_r.at[c],
            send_sem=s2.at[c, 3], recv_sem=r2.at[c, 2],
            device_id=(at_far_outer,), device_id_type=MESH,
        )

    def union_to_far(c, slot):
        return pltpu.make_async_remote_copy(
            src_ref=union_s.at[c], dst_ref=union_r.at[c, slot],
            send_sem=s2.at[c, 4], recv_sem=r2.at[c, 3 + slot],
            device_id=(at_far_inner,), device_id_type=MESH,
        )

    def back_to_mate(c):
        return along(c, 5, back_s.at[c], back_r.at[c], at_mate)

    def pass_to_mate(c):
        return along(c, 6, pass_s.at[c], pass_r.at[c], at_mate)

    parity = lax.rem(plane, 2)

    def columns(c):
        return pl.ds(pl.multiple_of(c * wide, wide), wide)

    live_count = live[0]
    loads[0].wait()
    step = rows // 4
    for t in range(rows // step):
        index = lax.broadcasted_iota(jnp.int32, (step, hidden), 0) + t * step
        part = saved_v[t * step : (t + 1) * step, :].astype(f32)
        part = jnp.where(index < live_count, part, 0.0)
        saved_t[:, t * step : (t + 1) * step] = part.astype(bf16).T

    loads[1].wait()

    def multiply(c):
        grad_v[...] = jnp.dot(saved_t[...], cot_v[:, columns(c)], preferred_element_type=f32)
        for s in range(GROUP):
            parts = [
                grad_v[(p * GROUP + s) * share : (p * GROUP + s + 1) * share, :]
                for p in range(planes)
            ]
            xy_s[c, s] = jnp.concatenate(parts, axis=0).astype(bf16)
        send_xy(c)

    def turn_back(t):
        few = rows // CHUNKS
        at = pl.ds(pl.multiple_of(t * few, few), few)
        index = lax.broadcasted_iota(jnp.int32, (few, hidden), 0) + t * few
        out = contract_cols(cot_v[at, :], weights_v[...])
        ig_v[at, :] = jnp.where(index < live_count, out, 0.0).astype(bf16)

    holder_at, next_at = experts, experts + devices
    place_at = experts + 2 * devices
    union_at = 3 * experts + 2 * devices

    def span(first_slot, slots):
        return table[holder_at + first_slot], table[holder_at + first_slot + slots - 1]

    def taken(e, held, most_held):
        first, last = held
        here = jnp.where(e >= first, 1.0, 0.0) * jnp.where(e <= last, 1.0, 0.0)
        return jnp.clip(e - first, 0, most_held - 1), here

    held_own = span(plane * GROUP, GROUP)
    held_mate = span(mate * GROUP, GROUP)
    held_side = span(side * 2 * GROUP, 2 * GROUP)
    held_far = span(far * 2 * GROUP, 2 * GROUP)

    def combine(c):
        half_to_mate(c).wait_recv()
        for i in range(2):
            for k in range(GROUP):
                half_v[i, k] = half_r[c, i, k]

        @pl.loop(0, most)
        def _(q):
            e = held_side[0] + q
            mine, mine_here = taken(e, held_own, GROUP)
            theirs, theirs_here = taken(e, held_mate, GROUP)
            for i in range(2):
                total = half_s[c, i, mine].astype(f32) * mine_here
                total = total + half_v[i, theirs].astype(f32) * theirs_here
                cross_s[c, i, q] = total.astype(bf16)

        across_inner(c).start()
        across_outer(c).start()

    def reduce(c):
        arrived_xy(c)
        for p in range(planes):
            total = jnp.zeros((share, wide), f32)
            for s in range(GROUP):
                now = plane * GROUP + s
                if s:
                    same = table[holder_at + now] == table[holder_at + now - 1]
                    total = total * jnp.where(same, 1.0, 0.0)
                total = total + xy_r[c, s].astype(f32)[p * share : (p + 1) * share, :]
                sums[p, s] = total.astype(bf16)
        for k in range(GROUP):
            e = jnp.minimum(held_own[0] + k, experts - 1)
            last = jnp.clip(table[e] - 1 - plane * GROUP, 0, GROUP - 1)
            half_s[c, 0, k] = sums[far_inner, last]
            half_s[c, 1, k] = sums[far_outer, last]
            mate_s[c, k] = sums[mate, last]
            own_v[c, k] = sums[plane, last]

        @pl.when(jnp.logical_not(is_inner))
        def _():
            half_to_mate(c).start()

        to_mate(c).start()

    for c in range(2):
        multiply(c)
    loads[2].wait()

    @pl.loop(2, CHUNKS + 3)
    def _(c):
        @pl.when(c < CHUNKS)
        def _():
            multiply(c)

        @pl.when(c < CHUNKS + 2)
        def _():
            reduce(c - 2)

        @pl.when((c > 2) & is_inner)
        def _():
            combine(c - 3)

        @pl.when(c < CHUNKS + 2)
        def _():
            turn_back(c - 2)

    ig_store = pltpu.make_async_copy(ig_v, ig_out, load_sem.at[6])
    ig_store.start()

    for load in loads[3:]:
        load.wait()

    @pl.loop(0, CHUNKS)
    def _(c):
        sent_xy(c)

    def update(c):
        to_mate(c).wait_recv()
        across_inner(c).wait_recv()
        for k in range(GROUP):
            mate_v[k] = mate_r[c, k]
        for k in range(most):
            cross_v[k] = cross_r[c, k]
        cols = columns(c)

        @pl.loop(0, experts)
        def _(e):
            at_own, own_here = taken(e, held_own, GROUP)
            at_next, next_here = taken(e, held_mate, GROUP)
            at_far, far_here = taken(e, held_far, most)
            grads = own_v[c, at_own].astype(f32) * own_here
            grads = grads + mate_v[at_next].astype(f32) * next_here
            grads = grads + cross_v[at_far].astype(f32) * far_here
            new, one, two = adam(
                grads,
                master_v[e, :, cols],
                moment1_v[e, :, cols].astype(f32),
                moment2_v[e, :, cols].astype(f32),
            )
            master_v[e, :, cols] = new
            moment1_v[e, :, cols] = one.astype(bf16)
            moment2_v[e, :, cols] = two.astype(bf16)
            fresh[c, e] = new.astype(bf16)

        for q in range(most):
            union_s[c, q] = fresh[c, table[union_at + far * (devices // 2) + q]]
        union_to_far(c, parity).start()
        for s in range(GROUP):
            back_s[c, s] = fresh[c, table[next_at + mate * GROUP + s]]
        back_to_mate(c).start()

    def hand_on(c):
        for i in range(2):
            union_to_far(c, i).wait_recv()
        for i in range(2):
            for q in range(most):
                union_v[i, q] = union_r[c, i, q]
        for s in range(GROUP):
            place = table[place_at + side * experts + table[next_at + mate * GROUP + s]]
            for i in range(2):
                pass_s[c, i, s] = union_v[i, place]
        pass_to_mate(c).start()
        for s in range(GROUP):
            place = table[place_at + side * experts + table[next_at + plane * GROUP + s]]
            for i in range(2):
                gather_v[2 * far + i, s] = union_v[i, place]

    def scatter(c):
        back_to_mate(c).wait_recv()
        for s in range(GROUP):
            gather_v[plane, s] = fresh[c, table[next_at + plane * GROUP + s]]
            gather_v[mate, s] = back_r[c, s]
        for s in range(GROUP):
            parts = [gather_v[p, s].astype(f32) for p in range(planes)]
            nxy_s[c, s] = jnp.concatenate(parts, axis=0).astype(bf16)
        send_nxy(c)

    @pl.loop(0, CHUNKS + 2)
    def _(c):
        @pl.when(c < CHUNKS)
        def _():
            update(c)

        @pl.when((c > 0) & (c <= CHUNKS) & is_inner)
        def _():
            hand_on(c - 1)
            scatter(c - 1)

        @pl.when((c > 1) & jnp.logical_not(is_inner))
        def _():
            pass_to_mate(c - 2).wait_recv()
            for i in range(2):
                for s in range(GROUP):
                    gather_v[2 * far + i, s] = pass_r[c - 2, i, s]
            scatter(c - 2)

    stores = [
        pltpu.make_async_copy(a, b, load_sem.at[7 + i])
        for i, (a, b) in enumerate(
            [(master_v, master_out), (moment1_v, moment1_out), (moment2_v, moment2_out)]
        )
    ]
    for store in stores:
        store.start()

    def store_next(c):
        cols = columns(c)
        return pltpu.make_async_copy(next_v.at[:, cols], next_out.at[:, cols], s5.at[c])

    @pl.loop(0, CHUNKS)
    def _(c):
        arrived_nxy(c)
        for p in range(planes):
            for s in range(0, GROUP, 2):
                pair = [
                    nxy_r[c, s + i].astype(f32)[p * share : (p + 1) * share, :] for i in range(2)
                ]
                at = (p * GROUP + s) * share
                next_v[at : at + 2 * share, columns(c)] = jnp.concatenate(pair, axis=0).astype(bf16)
        store_next(c).start()

    @pl.loop(0, CHUNKS)
    def _(c):
        to_mate(c).wait_send()
        union_to_far(c, parity).wait_send()
        back_to_mate(c).wait_send()
        sent_nxy(c)
        store_next(c).wait()

        @pl.when(is_inner)
        def _():
            across_inner(c).wait_send()
            across_outer(c).wait_send()
            pass_to_mate(c).wait_send()

        @pl.when(jnp.logical_not(is_inner))
        def _():
            half_to_mate(c).wait_send()

    for done in [ig_store] + stores:
        done.wait()


def fused(most, number, table, live, saved, cot, weights, master, moment1, moment2):
    experts, share, width = master.shape
    rows, hidden = saved.shape
    wide = width // CHUNKS
    bf16, f32 = jnp.bfloat16, jnp.float32
    vmem = pltpu.VMEM
    dma = pltpu.SemaphoreType.DMA
    anywhere = pl.BlockSpec(memory_space=pl.ANY)
    scalars = pl.BlockSpec(memory_space=pltpu.SMEM)
    across = vmem((CHUNKS, GROUP, PLANES * share, wide), bf16)
    blocks = lambda *lead: vmem((*lead, share, wide), bf16)
    return pl.pallas_call(
        functools.partial(kernel, most),
        out_shape=(
            jax.ShapeDtypeStruct((rows, hidden), bf16),
            jax.ShapeDtypeStruct(master.shape, f32),
            jax.ShapeDtypeStruct(moment1.shape, bf16),
            jax.ShapeDtypeStruct(moment2.shape, bf16),
            jax.ShapeDtypeStruct((hidden, width), bf16),
        ),
        in_specs=[scalars] * 2 + [anywhere] * 6,
        out_specs=(anywhere,) * 5,
        scratch_shapes=[
            vmem((rows, hidden), bf16),
            vmem((hidden, rows), bf16),
            vmem((rows, width), bf16),
            vmem((hidden, width), bf16),
            vmem(master.shape, f32),
            vmem(moment1.shape, bf16),
            vmem(moment2.shape, bf16),
            vmem((hidden, wide), f32),
            blocks(PLANES, GROUP),
            blocks(CHUNKS, experts),
            blocks(CHUNKS, GROUP), blocks(2, GROUP), blocks(GROUP),
            blocks(most), blocks(2, most), blocks(PLANES, GROUP),
            across, across,
            blocks(CHUNKS, 2, GROUP), blocks(CHUNKS, 2, GROUP),
            blocks(CHUNKS, GROUP), blocks(CHUNKS, GROUP),
            blocks(CHUNKS, 2, most), blocks(CHUNKS, most),
            blocks(CHUNKS, most), blocks(CHUNKS, 2, most),
            blocks(CHUNKS, GROUP), blocks(CHUNKS, GROUP),
            blocks(CHUNKS, 2, GROUP), blocks(CHUNKS, 2, GROUP),
            across,
            dma((11,)),
            dma((CHUNKS, GROUP)), dma((CHUNKS, GROUP)),
            dma((CHUNKS, 7)), dma((CHUNKS, 7)),
            dma((CHUNKS, GROUP)), dma((CHUNKS, GROUP)),
            dma((CHUNKS,)),
        ],
        compiler_params=pltpu.CompilerParams(
            collective_id=number, has_side_effects=True, vmem_limit_bytes=50 * 1024 * 1024
        ),
        cost_estimate=pl.CostEstimate(
            flops=4 * rows * hidden * width, bytes_accessed=26 << 20, transcendentals=0
        ),
        name=f"moe_step_{most}",
    )(table, live, saved, cot, weights, master, moment1, moment2)


def exchanged(saved, cotangent, weights, counts, live_rows, next_map, master, moment1, moment2):
    devices = lax.axis_size("dev")
    table, distinct = tables(counts, next_map)
    args = (table, live_rows, saved[0], cotangent[0], weights[0], master, moment1, moment2)
    outs = lax.cond(
        distinct[0] <= FEW,
        functools.partial(fused, FEW, 0),
        functools.partial(fused, devices // 2, 1),
        *args,
    )
    return (outs[0][None], outs[1], outs[2], outs[3], outs[4][None])


def solution(mesh):
    devices = mesh.shape["dev"]

    def per_device(*args):
        share, width = args[6].shape[1:]
        takes = devices == PLANES * GROUP and GROUP >= MOST and share % 8 == 0
        takes = takes and width % (CHUNKS * 128) == 0 and args[0].shape[1] % (CHUNKS * 16) == 0
        return (exchanged if takes else plain)(*args)

    placed = (
        P("dev", None, None),
        P("dev", None, None),
        P("dev", None, None),
        P(),
        P("dev"),
        P(),
        P(None, "dev", None),
        P(None, "dev", None),
        P(None, "dev", None),
    )
    return jax.shard_map(
        per_device,
        mesh=mesh,
        in_specs=placed,
        out_specs=(
            P("dev", None, None),
            P(None, "dev", None),
            P(None, "dev", None),
            P(None, "dev", None),
            P("dev", None, None),
        ),
        check_vma=False,
    )
```

```python
import functools

import jax
import jax.numpy as jnp
from jax import lax
from jax.experimental import pallas as pl
from jax.experimental.pallas import tpu as pltpu
from jax.sharding import PartitionSpec as P

LEARN_RATE = 0.001
DECAY_RATE = 0.1
BETA_ONE = 0.9
BETA_TWO = 0.95
BIAS_ONE = 1.0 - 0.9**20
BIAS_TWO = 1.0 - 0.95**20
EPSILON = 1e-08
GROUP = 8
CHUNKS = 16
PLANES = 4
MOST = 8
WIDTHS = (11, 13)
MESH = pl.DeviceIdType.MESH


def contract_rows(left, right):
    return lax.dot_general(
        left, right, (((0,), (0,)), ((), ())), preferred_element_type=jnp.float32
    )


def contract_cols(left, right):
    return lax.dot_general(
        left, right, (((1,), (1,)), ((), ())), preferred_element_type=jnp.float32
    )


def adam(grads, master, moment1, moment2):
    first = BETA_ONE * moment1 + (1.0 - BETA_ONE) * grads
    second = BETA_TWO * moment2 + (1.0 - BETA_TWO) * grads * grads
    update = first / BIAS_ONE / (jnp.sqrt(second / BIAS_TWO) + EPSILON) + DECAY_RATE * master
    return master - LEARN_RATE * update, first, second


def plain(saved, cotangent, weights, counts, live_rows, next_map, master, moment1, moment2):
    hidden_rows, cot_rows, slot_weights = saved[0], cotangent[0], weights[0]
    devices = lax.axis_size("dev")
    expert_count, share_rows, model_width = master.shape
    row_index = jnp.arange(hidden_rows.shape[0], dtype=jnp.int32)
    masked = jnp.where((row_index < live_rows[0])[:, None], cot_rows, jnp.zeros_like(cot_rows))
    input_grads = contract_cols(masked, slot_weights).astype(jnp.bfloat16)
    slot_grads = contract_rows(hidden_rows, masked).astype(jnp.bfloat16)
    slot_index = jnp.arange(devices, dtype=jnp.int32)
    bounds = jnp.cumsum(counts)
    holders = jnp.sum((bounds[None, :] <= slot_index[:, None]).astype(jnp.int32), axis=1)
    selector = (jnp.arange(expert_count, dtype=jnp.int32)[:, None] == holders[None, :]).astype(
        jnp.bfloat16
    )
    received = lax.all_to_all(slot_grads, "dev", split_axis=0, concat_axis=0, tiled=True)
    pieces = received.reshape(devices, share_rows, model_width)
    expert_grads = jnp.einsum("es,src->erc", selector, pieces, preferred_element_type=jnp.float32)
    master_out, first, second = adam(
        expert_grads, master, moment1.astype(jnp.float32), moment2.astype(jnp.float32)
    )
    outgoing = jnp.take(master_out.astype(jnp.bfloat16), next_map, axis=0)
    outgoing = outgoing.reshape(devices * share_rows, model_width)
    arriving = lax.all_to_all(outgoing, "dev", split_axis=0, concat_axis=0, tiled=True)
    return (
        input_grads[None],
        master_out,
        first.astype(jnp.bfloat16),
        second.astype(jnp.bfloat16),
        arriving[None],
    )


def plan(counts, next_map, table, distinct):
    experts, devices = counts.shape[0], next_map.shape[0]
    half = devices // 2
    holder_at, next_at = experts, experts + devices
    place_at = experts + 2 * devices
    union_at = place_at + 2 * experts

    def bound(e, total):
        table[e] = total + counts[e]
        return total + counts[e]

    lax.fori_loop(0, experts, bound, jnp.int32(0))

    def clear(i, _):
        table[place_at + i] = 0
        return _

    lax.fori_loop(0, 2 * experts + devices, clear, jnp.int32(0))

    def holder(s, e):
        e = jnp.minimum(jnp.where(table[e] <= s, e + 1, e), experts - 1)
        table[holder_at + s] = e
        e_next = next_map[s]
        table[next_at + s] = e_next
        table[place_at + (s // half) * experts + e_next] = 1
        return e

    lax.fori_loop(0, devices, holder, jnp.int32(0))
    most = jnp.maximum(
        table[holder_at + half - 1] - table[holder_at],
        table[holder_at + devices - 1] - table[holder_at + half],
    )
    most = most + 1
    for h in range(2):

        def rank(e, held, h=h):
            here = table[place_at + h * experts + e]
            table[place_at + h * experts + e] = held

            @pl.when(here == 1)
            def _():
                table[union_at + h * half + held] = e

            return held + here

        most = jnp.maximum(most, lax.fori_loop(0, experts, rank, jnp.int32(0)))
    distinct[0] = most


def tables(counts, next_map):
    experts, devices = counts.shape[0], next_map.shape[0]
    scalars = pl.BlockSpec(memory_space=pltpu.SMEM)
    return pl.pallas_call(
        plan,
        out_shape=(
            jax.ShapeDtypeStruct((3 * experts + 3 * devices,), jnp.int32),
            jax.ShapeDtypeStruct((1,), jnp.int32),
        ),
        in_specs=[scalars] * 2,
        out_specs=(scalars,) * 2,
        name="plan",
    )(counts, next_map)


def kernel(
    most,
    table, live, saved, cot, weights, master, moment1, moment2,
    ig_out, master_out, moment1_out, moment2_out, next_out,
    saved_v, saved_t, cot_v, weights_v, master_v, moment1_v, moment2_v,
    grad_v, sums, fresh, own_v, half_v, mate_v, cross_v, union_v, gather_v,
    xy_s, xy_r, half_s, half_r, mate_s, mate_r, cross_s, cross_r,
    union_s, union_r, back_s, back_r, pass_s, pass_r, nxy_r,
    load_sem, s1, r1, s2, r2, s4, r4, s5,
):
    me = lax.axis_index("dev")
    plane, spot = me // GROUP, lax.rem(me, GROUP)
    planes, devices = PLANES, PLANES * GROUP
    ig_v, next_v, nxy_s = saved_v, weights_v, xy_s
    side = plane // 2
    inner = 1 + side
    is_inner = plane == inner
    mate = 2 * side + 1 - lax.rem(plane, 2)
    far = 1 - side
    far_inner, far_outer = 2 - side, 3 - 3 * side
    at_mate, at_far_inner, at_far_outer = (
        p * GROUP + spot for p in (mate, far_inner, far_outer)
    )
    experts, share, width = master_v.shape
    rows, hidden = saved_v.shape
    wide = width // CHUNKS
    f32, bf16 = jnp.float32, jnp.bfloat16

    loads = [
        pltpu.make_async_copy(a, b, load_sem.at[i])
        for i, (a, b) in enumerate(
            [
                (saved, saved_v), (cot, cot_v), (weights, weights_v),
                (master, master_v), (moment1, moment1_v), (moment2, moment2_v),
            ]
        )
    ]
    for load in loads:
        load.start()

    barrier = pltpu.get_barrier_semaphore()
    peers = [plane * GROUP + lax.rem(spot + o, GROUP) for o in range(1, GROUP)]
    peers += [lax.rem(plane + o, planes) * GROUP + spot for o in range(1, planes)]
    for peer in peers:
        pl.semaphore_signal(barrier, inc=1, device_id=(peer,), device_id_type=MESH)
    pl.semaphore_wait(barrier, len(peers))

    def exchange(src, dst, ssem, rsem, mine, count, device_of):
        def remote(c, other, slot):
            return pltpu.make_async_remote_copy(
                src_ref=src.at[c, other], dst_ref=dst.at[c, slot],
                send_sem=ssem.at[c, other], recv_sem=rsem.at[c, slot],
                device_id=(device_of(other),), device_id_type=MESH,
            )

        def own(c):
            return pltpu.make_async_copy(src.at[c, mine], dst.at[c, mine], rsem.at[c, mine])

        others = [lax.rem(mine + o, count) for o in range(1, count)]

        def send(c):
            for other in others:
                remote(c, other, mine).start()
            own(c).start()

        def arrived(c):
            for other in others:
                remote(c, other, other).wait_recv()
            own(c).wait()

        def sent(c):
            for other in others:
                remote(c, other, mine).wait_send()

        return send, arrived, sent

    in_plane = lambda s: plane * GROUP + s
    send_xy, arrived_xy, sent_xy = exchange(xy_s, xy_r, s1, r1, spot, GROUP, in_plane)
    send_nxy, arrived_nxy, sent_nxy = exchange(nxy_s, nxy_r, s4, r4, spot, GROUP, in_plane)

    def along(c, number, src, dst, device):
        return pltpu.make_async_remote_copy(
            src_ref=src, dst_ref=dst, send_sem=s2.at[c, number], recv_sem=r2.at[c, number],
            device_id=(device,), device_id_type=MESH,
        )

    def to_mate(c):
        return along(c, 0, mate_s.at[c], mate_r.at[c], at_mate)

    def half_to_mate(c):
        return along(c, 1, half_s.at[c], half_r.at[c], at_mate)

    def across_inner(c):
        return along(c, 2, cross_s.at[c, 0], cross_r.at[c], at_far_inner)

    def across_outer(c):
        return pltpu.make_async_remote_copy(
            src_ref=cross_s.at[c, 1], dst_ref=cross_r.at[c],
            send_sem=s2.at[c, 3], recv_sem=r2.at[c, 2],
            device_id=(at_far_outer,), device_id_type=MESH,
        )

    def union_to_far(c, slot):
        return pltpu.make_async_remote_copy(
            src_ref=union_s.at[c], dst_ref=union_r.at[c, slot],
            send_sem=s2.at[c, 4], recv_sem=r2.at[c, 3 + slot],
            device_id=(at_far_inner,), device_id_type=MESH,
        )

    def back_to_mate(c):
        return along(c, 5, back_s.at[c], back_r.at[c], at_mate)

    def pass_to_mate(c):
        return along(c, 6, pass_s.at[c], pass_r.at[c], at_mate)

    parity = lax.rem(plane, 2)

    def columns(c):
        return pl.ds(pl.multiple_of(c * wide, wide), wide)

    live_count = live[0]
    loads[0].wait()
    step = rows // 4
    for t in range(rows // step):
        index = lax.broadcasted_iota(jnp.int32, (step, hidden), 0) + t * step
        part = saved_v[t * step : (t + 1) * step, :].astype(f32)
        part = jnp.where(index < live_count, part, 0.0)
        saved_t[:, t * step : (t + 1) * step] = part.astype(bf16).T

    loads[1].wait()

    def multiply(c):
        grad_v[...] = jnp.dot(saved_t[...], cot_v[:, columns(c)], preferred_element_type=f32)
        for s in range(GROUP):
            parts = [
                grad_v[(p * GROUP + s) * share : (p * GROUP + s + 1) * share, :]
                for p in range(planes)
            ]
            xy_s[c, s] = jnp.concatenate(parts, axis=0).astype(bf16)
        send_xy(c)

    def turn_back(t):
        few = rows // CHUNKS
        at = pl.ds(pl.multiple_of(t * few, few), few)
        index = lax.broadcasted_iota(jnp.int32, (few, hidden), 0) + t * few
        out = contract_cols(cot_v[at, :], weights_v[...])
        ig_v[at, :] = jnp.where(index < live_count, out, 0.0).astype(bf16)

    holder_at, next_at = experts, experts + devices
    place_at = experts + 2 * devices
    union_at = 3 * experts + 2 * devices

    def span(first_slot, slots):
        return table[holder_at + first_slot], table[holder_at + first_slot + slots - 1]

    def taken(e, held, most_held):
        first, last = held
        here = jnp.where(e >= first, 1.0, 0.0) * jnp.where(e <= last, 1.0, 0.0)
        return jnp.clip(e - first, 0, most_held - 1), here

    held_own = span(plane * GROUP, GROUP)
    held_mate = span(mate * GROUP, GROUP)
    held_side = span(side * 2 * GROUP, 2 * GROUP)
    held_far = span(far * 2 * GROUP, 2 * GROUP)

    def combine(c):
        half_to_mate(c).wait_recv()
        for i in range(2):
            for k in range(GROUP):
                half_v[i, k] = half_r[c, i, k]

        @pl.loop(0, most)
        def _(q):
            e = held_side[0] + q
            mine, mine_here = taken(e, held_own, GROUP)
            theirs, theirs_here = taken(e, held_mate, GROUP)
            for i in range(2):
                total = half_s[c, i, mine].astype(f32) * mine_here
                total = total + half_v[i, theirs].astype(f32) * theirs_here
                cross_s[c, i, q] = total.astype(bf16)

        across_inner(c).start()
        across_outer(c).start()

    def reduce(c):
        arrived_xy(c)
        for p in range(planes):
            total = jnp.zeros((share, wide), f32)
            for s in range(GROUP):
                now = plane * GROUP + s
                if s:
                    same = table[holder_at + now] == table[holder_at + now - 1]
                    total = total * jnp.where(same, 1.0, 0.0)
                total = total + xy_r[c, s].astype(f32)[p * share : (p + 1) * share, :]
                sums[p, s] = total.astype(bf16)
        for k in range(GROUP):
            e = jnp.minimum(held_own[0] + k, experts - 1)
            last = jnp.clip(table[e] - 1 - plane * GROUP, 0, GROUP - 1)
            half_s[c, 0, k] = sums[far_inner, last]
            half_s[c, 1, k] = sums[far_outer, last]
            mate_s[c, k] = sums[mate, last]
            own_v[c, k] = sums[plane, last]

        @pl.when(jnp.logical_not(is_inner))
        def _():
            half_to_mate(c).start()

        @pl.when(is_inner)
        def _():
            to_mate(c).start()

    for c in range(2):
        multiply(c)
    loads[2].wait()

    @pl.loop(2, CHUNKS + 3)
    def _(c):
        @pl.when(c < CHUNKS)
        def _():
            multiply(c)

        @pl.when(c < CHUNKS + 2)
        def _():
            reduce(c - 2)

        @pl.when((c > 2) & is_inner)
        def _():
            combine(c - 3)

        @pl.when(c < CHUNKS + 2)
        def _():
            turn_back(c - 2)

    @pl.when(jnp.logical_not(is_inner))
    def _():
        @pl.loop(0, CHUNKS)
        def _(c):
            to_mate(c).start()

    ig_store = pltpu.make_async_copy(ig_v, ig_out, load_sem.at[6])
    ig_store.start()

    for load in loads[3:]:
        load.wait()

    @pl.loop(0, CHUNKS)
    def _(c):
        sent_xy(c)

    def update(c):
        to_mate(c).wait_recv()
        across_inner(c).wait_recv()
        for k in range(GROUP):
            mate_v[k] = mate_r[c, k]
        for k in range(most):
            cross_v[k] = cross_r[c, k]
        cols = columns(c)

        @pl.loop(0, experts)
        def _(e):
            at_own, own_here = taken(e, held_own, GROUP)
            at_next, next_here = taken(e, held_mate, GROUP)
            at_far, far_here = taken(e, held_far, most)
            grads = own_v[c, at_own].astype(f32) * own_here
            grads = grads + mate_v[at_next].astype(f32) * next_here
            grads = grads + cross_v[at_far].astype(f32) * far_here
            new, one, two = adam(
                grads,
                master_v[e, :, cols],
                moment1_v[e, :, cols].astype(f32),
                moment2_v[e, :, cols].astype(f32),
            )
            master_v[e, :, cols] = new
            moment1_v[e, :, cols] = one.astype(bf16)
            moment2_v[e, :, cols] = two.astype(bf16)
            fresh[c, e] = new.astype(bf16)

        for q in range(most):
            union_s[c, q] = fresh[c, table[union_at + far * (devices // 2) + q]]
        union_to_far(c, parity).start()
        for s in range(GROUP):
            back_s[c, s] = fresh[c, table[next_at + mate * GROUP + s]]
        back_to_mate(c).start()

    def hand_on(c):
        for i in range(2):
            union_to_far(c, i).wait_recv()
        for i in range(2):
            for q in range(most):
                union_v[i, q] = union_r[c, i, q]
        for s in range(GROUP):
            place = table[place_at + side * experts + table[next_at + mate * GROUP + s]]
            for i in range(2):
                pass_s[c, i, s] = union_v[i, place]
        pass_to_mate(c).start()
        for s in range(GROUP):
            place = table[place_at + side * experts + table[next_at + plane * GROUP + s]]
            for i in range(2):
                gather_v[2 * far + i, s] = union_v[i, place]

    def scatter(c):
        back_to_mate(c).wait_recv()
        for s in range(GROUP):
            gather_v[plane, s] = fresh[c, table[next_at + plane * GROUP + s]]
            gather_v[mate, s] = back_r[c, s]
        for s in range(GROUP):
            parts = [gather_v[p, s].astype(f32) for p in range(planes)]
            nxy_s[c, s] = jnp.concatenate(parts, axis=0).astype(bf16)
        send_nxy(c)

    @pl.loop(0, CHUNKS + 2)
    def _(c):
        @pl.when(c < CHUNKS)
        def _():
            update(c)

        @pl.when((c > 0) & (c <= CHUNKS) & is_inner)
        def _():
            hand_on(c - 1)
            scatter(c - 1)

        @pl.when((c > 1) & jnp.logical_not(is_inner))
        def _():
            pass_to_mate(c - 2).wait_recv()
            for i in range(2):
                for s in range(GROUP):
                    gather_v[2 * far + i, s] = pass_r[c - 2, i, s]
            scatter(c - 2)

    stores = [
        pltpu.make_async_copy(a, b, load_sem.at[7 + i])
        for i, (a, b) in enumerate(
            [(master_v, master_out), (moment1_v, moment1_out), (moment2_v, moment2_out)]
        )
    ]
    for store in stores:
        store.start()

    def store_next(c):
        cols = columns(c)
        return pltpu.make_async_copy(next_v.at[:, cols], next_out.at[:, cols], s5.at[c])

    @pl.loop(0, CHUNKS)
    def _(c):
        arrived_nxy(c)
        for p in range(planes):
            for s in range(0, GROUP, 2):
                pair = [
                    nxy_r[c, s + i].astype(f32)[p * share : (p + 1) * share, :] for i in range(2)
                ]
                at = (p * GROUP + s) * share
                next_v[at : at + 2 * share, columns(c)] = jnp.concatenate(pair, axis=0).astype(bf16)
        store_next(c).start()

    @pl.loop(0, CHUNKS)
    def _(c):
        to_mate(c).wait_send()
        union_to_far(c, parity).wait_send()
        back_to_mate(c).wait_send()
        sent_nxy(c)
        store_next(c).wait()

        @pl.when(is_inner)
        def _():
            across_inner(c).wait_send()
            across_outer(c).wait_send()
            pass_to_mate(c).wait_send()

        @pl.when(jnp.logical_not(is_inner))
        def _():
            half_to_mate(c).wait_send()

    for done in [ig_store] + stores:
        done.wait()


def fused(most, number, table, live, saved, cot, weights, master, moment1, moment2):
    experts, share, width = master.shape
    rows, hidden = saved.shape
    wide = width // CHUNKS
    bf16, f32 = jnp.bfloat16, jnp.float32
    vmem = pltpu.VMEM
    dma = pltpu.SemaphoreType.DMA
    anywhere = pl.BlockSpec(memory_space=pl.ANY)
    scalars = pl.BlockSpec(memory_space=pltpu.SMEM)
    across = vmem((CHUNKS, GROUP, PLANES * share, wide), bf16)
    blocks = lambda *lead: vmem((*lead, share, wide), bf16)
    return pl.pallas_call(
        functools.partial(kernel, most),
        out_shape=(
            jax.ShapeDtypeStruct((rows, hidden), bf16),
            jax.ShapeDtypeStruct(master.shape, f32),
            jax.ShapeDtypeStruct(moment1.shape, bf16),
            jax.ShapeDtypeStruct(moment2.shape, bf16),
            jax.ShapeDtypeStruct((hidden, width), bf16),
        ),
        in_specs=[scalars] * 2 + [anywhere] * 6,
        out_specs=(anywhere,) * 5,
        scratch_shapes=[
            vmem((rows, hidden), bf16),
            vmem((hidden, rows), bf16),
            vmem((rows, width), bf16),
            vmem((hidden, width), bf16),
            vmem(master.shape, f32),
            vmem(moment1.shape, bf16),
            vmem(moment2.shape, bf16),
            vmem((hidden, wide), f32),
            blocks(PLANES, GROUP),
            blocks(CHUNKS, experts),
            blocks(CHUNKS, GROUP), blocks(2, GROUP), blocks(GROUP),
            blocks(most), blocks(2, most), blocks(PLANES, GROUP),
            across, across,
            blocks(CHUNKS, 2, GROUP), blocks(CHUNKS, 2, GROUP),
            blocks(CHUNKS, GROUP), blocks(CHUNKS, GROUP),
            blocks(CHUNKS, 2, most), blocks(CHUNKS, most),
            blocks(CHUNKS, most), blocks(CHUNKS, 2, most),
            blocks(CHUNKS, GROUP), blocks(CHUNKS, GROUP),
            blocks(CHUNKS, 2, GROUP), blocks(CHUNKS, 2, GROUP),
            across,
            dma((11,)),
            dma((CHUNKS, GROUP)), dma((CHUNKS, GROUP)),
            dma((CHUNKS, 7)), dma((CHUNKS, 7)),
            dma((CHUNKS, GROUP)), dma((CHUNKS, GROUP)),
            dma((CHUNKS,)),
        ],
        compiler_params=pltpu.CompilerParams(
            collective_id=number, has_side_effects=True, vmem_limit_bytes=50 * 1024 * 1024
        ),
        cost_estimate=pl.CostEstimate(
            flops=4 * rows * hidden * width, bytes_accessed=26 << 20, transcendentals=0
        ),
        name=f"moe_step_{most}",
    )(table, live, saved, cot, weights, master, moment1, moment2)


def exchanged(saved, cotangent, weights, counts, live_rows, next_map, master, moment1, moment2):
    devices = lax.axis_size("dev")
    table, distinct = tables(counts, next_map)
    args = (table, live_rows, saved[0], cotangent[0], weights[0], master, moment1, moment2)
    widths = WIDTHS + (devices // 2,)
    which = sum((distinct[0] > width).astype(jnp.int32) for width in WIDTHS)
    outs = lax.switch(
        which, [functools.partial(fused, width, i) for i, width in enumerate(widths)], *args
    )
    return (outs[0][None], outs[1], outs[2], outs[3], outs[4][None])


def solution(mesh):
    devices = mesh.shape["dev"]

    def per_device(*args):
        share, width = args[6].shape[1:]
        takes = devices == PLANES * GROUP and GROUP >= MOST and share % 8 == 0
        takes = takes and width % (CHUNKS * 128) == 0 and args[0].shape[1] % (CHUNKS * 16) == 0
        return (exchanged if takes else plain)(*args)

    placed = (
        P("dev", None, None),
        P("dev", None, None),
        P("dev", None, None),
        P(),
        P("dev"),
        P(),
        P(None, "dev", None),
        P(None, "dev", None),
        P(None, "dev", None),
    )
    return jax.shard_map(
        per_device,
        mesh=mesh,
        in_specs=placed,
        out_specs=(
            P("dev", None, None),
            P(None, "dev", None),
            P(None, "dev", None),
            P(None, "dev", None),
            P("dev", None, None),
        ),
        check_vma=False,
    )
```
